32 devices in a mesh: ctx: 2 (over x), head: 4 (over y, core), exp: 4 (over z).
Axes of the slice: x: 2, y: 2, z: 4, core: 2. Of those that a mesh axis runs over, the one named last changes fastest.
Arguments:
- resid: bfloat16 [1024, 2048], P(('ctx', 'exp')), may hold values from -6 to 6
- queries: bfloat16 [1024, 4096], P(('ctx', 'exp'), 'head'), may hold values from -42 to 42
- rotated_key_value_pairs: bfloat16 [2, 1024, 512], P(None, ('ctx', 'exp'), 'head'), may hold values from -13 to 13
- doc_ids: int32 [1, 1024], P(None, ('ctx', 'exp')), may hold values from 0 to 5, never falling along the last dimension, each value on 1 to 768 neighbouring positions
- out_weight: bfloat16 [4096, 2048], P('head', ('ctx', 'exp')), may hold values from -0.09375 to 0.09375
- norm_gain: float32 [2048], replicated, may hold values from 0.1 to 1.9
- routes: int32 [1024, 8], P(('ctx', 'exp')), may hold values from 0 to 15, all different within a row; in each aligned block of 128 rows (0 to 127, 128 to 255, ...) at most 80 rows name the same one
- probs: float32 [1024, 8], P(('ctx', 'exp')), may hold values from 0.05 to 0.3
- w_gate: bfloat16 [16, 768, 2048], P(('ctx', 'exp'), None, 'head'), may hold values from -0.125 to 0.125
- w_up: bfloat16 [16, 768, 2048], P(('ctx', 'exp'), None, 'head'), may hold values from -0.125 to 0.125
- w_down: bfloat16 [16, 768, 2048], P(('ctx', 'exp'), None, 'head'), may hold values from -0.21875 to 0.21875
- cotangent: bfloat16 [1024, 2048], P(('ctx', 'exp')), may hold values from -6 to 6
Outputs:
- layer_out: bfloat16 [1024, 2048], P(('ctx', 'exp'), 'head')
- grad_gate: bfloat16 [16, 768, 2048], P(('ctx', 'exp'), None, 'head')
- grad_up: bfloat16 [16, 768, 2048], P(('ctx', 'exp'), None, 'head')
- grad_down: bfloat16 [16, 768, 2048], P(('ctx', 'exp'), None, 'head')
The draws below stay inside these ranges and needn't reach their ends.
Inputs may be any that keep to these rules, and one draw needn't show every extreme that they name: `routes`: in the rows of one index of ctx+exp (aligned blocks of 128 rows) no expert is named more than 80 times, a bound that some block reaches; a row names 8 different experts. `doc_ids`: ids never fall along positions; a document spans 1 to 768 positions, one exactly 768.
All inputs are finite; a program needn't handle non-finite values.
Results may differ from the reference program's by a relative error of at most 0.018.
Values may be sent and summed in bfloat16 or wider, within the bound.
A program may use at most 128 MiB of HBM per device.

```python
import math
import jax
import jax.numpy as jnp
import numpy as np
from jax import lax

D = 2048
QUERY_HEADS = 32
KEY_VALUE_HEADS = 4
HEAD_DIMENSION = 128
FF = 768
TOPK = 8
TOK_DEV = 128
DOCS = 6
EXPERTS = 16
WINDOW_TOKENS = 1024
CAP = 80
DOC_MOST = 768


def drawn_pair(key):
    key_unrotated = jnp.clip(jax.random.normal(jax.random.fold_in(key, 11), (WINDOW_TOKENS, KEY_VALUE_HEADS, HEAD_DIMENSION), jnp.float32), -4.0, 4.0)
    value_unprojected = jnp.clip(jax.random.normal(jax.random.fold_in(key, 12), (WINDOW_TOKENS, KEY_VALUE_HEADS * HEAD_DIMENSION), jnp.float32), -4.0, 4.0)
    query_noise = jnp.clip(jax.random.normal(jax.random.fold_in(key, 13), (WINDOW_TOKENS, QUERY_HEADS * HEAD_DIMENSION), jnp.float32), -4.0, 4.0)
    group_width = QUERY_HEADS // KEY_VALUE_HEADS
    half_window = WINDOW_TOKENS // 2
    earlier_keys = jnp.roll(key_unrotated, half_window, axis=0)
    later_half = (jnp.arange(WINDOW_TOKENS, dtype=jnp.int32) >= half_window).astype(jnp.float32)
    earlier_wide = jnp.broadcast_to(earlier_keys[:, :, None, :], (WINDOW_TOKENS, KEY_VALUE_HEADS, group_width, HEAD_DIMENSION)).reshape(WINDOW_TOKENS, QUERY_HEADS * HEAD_DIMENSION)
    query_raw = query_noise + 0.9 * later_half[:, None] * earlier_wide
    key_rotated_final = key_unrotated
    query_final = query_raw
    stacked_pairs = jnp.stack([key_rotated_final.reshape(WINDOW_TOKENS, KEY_VALUE_HEADS * HEAD_DIMENSION), value_unprojected], axis=0)
    return (query_final, stacked_pairs)


def draw_queries(key, part):
    return drawn_pair(key)[0].astype(jnp.bfloat16)


def draw_rotated_key_value_pairs(key, part):
    return drawn_pair(key)[1].astype(jnp.bfloat16)


def levels(key, dims, split, low, top_value):
    def one(axis_at, parts):
        draws = jax.random.uniform(jax.random.fold_in(jax.random.fold_in(key, 6), axis_at), (parts,), jnp.float32, low / len(split), top_value / len(split))
        return jnp.repeat(jnp.exp(draws), dims[axis_at] // parts).reshape((-1,) + (1,) * (len(dims) - axis_at - 1))

    level = one(*split[0])
    for cut in split[1:]:
        level = level * one(*cut)
    return level


def length_profile(number_of, total, most, skew):
    portions = [(1 << 20) // math.isqrt(standing ** skew) + 1 for standing in range(2, number_of + 1)]
    spare, holding = total - most - (number_of - 1), [1] * (number_of - 1)
    while spare > 0:
        free = [i for i in range(number_of - 1) if holding[i] < most]
        pool, left = sum([portions[i] for i in free]), spare
        for i in free:
            more = min(most - holding[i], max(1, left * portions[i] // pool), spare)
            holding[i] = holding[i] + more
            spare = spare - more
    return np.array([most] + holding)


def ragged(key, amount, total, reach, slope):
    if amount == 2:
        one = jax.random.randint(key, (), max(1, total - reach), min(reach, total - 1) + 1)
        return jnp.stack([one, total - one])
    lengths = jnp.asarray(length_profile(amount, total, reach, slope), jnp.int32)
    twos = (amount - 1) // 2
    donor, sink = lengths[1:1 + 2 * twos:2], lengths[2:2 + 2 * twos:2]
    slack = jnp.minimum(donor - 1, reach - sink)
    shifted = jax.random.randint(jax.random.fold_in(key, 1), (twos,), 0, 1 << 20) % (slack + 1)
    lengths = lengths.at[1:1 + 2 * twos:2].set(donor - shifted).at[2:2 + 2 * twos:2].set(sink + shifted)
    return lengths[jax.random.permutation(jax.random.fold_in(key, 2), amount)]


def assign_block(key, own, number, rows, count, top, limit, lean):
    order = jax.random.permutation(key, count)
    packed, ordinary = load_shares(count, rows * top, limit, lean, True), load_shares(count, rows * top, limit, lean, False)
    places = jnp.arange(count)

    def named(sizes, turn):
        used = int((sizes > 0).sum())
        fixed = max(1, used // 4)
        shifted = fixed + (places - fixed + turn * (used - fixed)) % max(1, count - fixed)
        return jnp.zeros((count,), jnp.int32).at[order[jnp.where(places < fixed, places, shifted)]].set(jnp.asarray(sizes, jnp.int32))

    sizes = jnp.where(number % 4 == 0, named(packed, number // 4), named(ordinary, number - number // 4 - 1))
    mixed = jax.random.permutation(jax.random.fold_in(own, 3), count)
    giver, sink = mixed[0:count // 2 * 2:2], mixed[1:count // 2 * 2:2]
    room = jnp.minimum(sizes[giver] - 1, limit - sizes[sink]) // 2
    room = jnp.where((giver == order[0]) | (sink == order[0]) | (sizes[sink] == 0), 0, jnp.maximum(room, 0))
    shifted = jax.random.randint(jax.random.fold_in(own, 4), (count // 2,), 0, 1 << 20) % (room + 1)
    sizes = sizes.at[giver].add(-shifted).at[sink].add(shifted)
    members = jnp.searchsorted(jnp.cumsum(sizes), jnp.arange(rows * top), side="right").astype(jnp.int32)
    listing = members.reshape(top, rows).T
    listing = listing[jax.random.permutation(jax.random.fold_in(own, 1), rows)]
    turn = jax.random.randint(jax.random.fold_in(own, 2), (rows, 1), 0, top)
    return jnp.take_along_axis(listing, (jnp.arange(top)[None, :] + turn) % top, axis=1)


def load_shares(number_of, total, limit, slope, full):
    loads = [(1 << 20) // math.isqrt(standing ** slope) + 1 for standing in range(1, number_of + 1)]
    largest = limit if full else min(limit, max(-(-total // number_of), total * loads[0] // sum(loads)))
    least = 1 if total - largest >= number_of - 1 else 0
    counts, surplus = [largest] + [least] * (number_of - 1), total - largest - least * (number_of - 1)
    while surplus > 0:
        candidates = [i for i in range(1, number_of) if counts[i] < largest] or [i for i in range(1, number_of) if counts[i] < limit]
        mass, remaining = sum([loads[i] for i in candidates]), surplus
        for i in candidates:
            more = min(limit - counts[i], max(1, remaining * loads[i] // mass), surplus)
            counts[i] = counts[i] + more
            surplus = surplus - more
    return np.array(counts)


def noise(own_key, extent, width, bound, split=(), held_as=jnp.bfloat16):
    drawn = width * jax.random.normal(own_key, extent, jnp.float32)
    if split:
        drawn = drawn * levels(own_key, extent, split, -0.22, 0.18)
    return jnp.clip(drawn, -bound, bound).astype(held_as)


def setup_inputs(seed: int = 0) -> dict:
    key_of = jax.random.split(jax.random.key(seed), 13)
    resid = noise(key_of[0], (WINDOW_TOKENS, D), 1.0, 6.0, ((0, 8),))
    queries = draw_queries(jax.random.fold_in(key_of[12], 71), 0)
    rotated_key_value_pairs = draw_rotated_key_value_pairs(jax.random.fold_in(key_of[12], 71), 0)
    doc_ids = jax.vmap(lambda own: jnp.searchsorted(jnp.cumsum(ragged(own, DOCS, WINDOW_TOKENS, DOC_MOST, 1)), jnp.arange(WINDOW_TOKENS), side="right"))(jax.random.split(key_of[3], 1)).reshape((1, WINDOW_TOKENS)).astype(jnp.int32)
    out_weight = noise(key_of[4], (QUERY_HEADS * HEAD_DIMENSION, D), (QUERY_HEADS * HEAD_DIMENSION) ** -0.5, 0.09375, ((0, 4), (1, 8)))
    norm_gain = jnp.clip(1.0 + 0.18 * jax.random.normal(key_of[5], (D,), jnp.float32), 0.1, 1.9)
    routes_keys = jax.random.split(jax.random.fold_in(key_of[6], 1), WINDOW_TOKENS // TOK_DEV)
    routes_turns = jax.random.permutation(jax.random.fold_in(key_of[6], 3), WINDOW_TOKENS // TOK_DEV)
    routes = jax.vmap(lambda own, number: assign_block(jax.random.fold_in(key_of[6], 2), own, number, TOK_DEV, EXPERTS, TOPK, CAP, 2))(routes_keys, routes_turns).reshape((WINDOW_TOKENS, TOPK))
    probs = jnp.clip(0.05 + 0.25 * jax.random.uniform(key_of[7], (WINDOW_TOKENS, TOPK), jnp.float32) ** levels(key_of[7], (WINDOW_TOKENS, TOPK), ((0, 8),), -0.2, 0.2), 0.05, 0.3)
    w_gate = noise(key_of[8], (EXPERTS, FF, D), D ** -0.5, 0.125, ((0, 8), (2, 4)))
    w_up = noise(key_of[9], (EXPERTS, FF, D), D ** -0.5, 0.125, ((0, 8), (2, 4)))
    w_down = noise(key_of[10], (EXPERTS, FF, D), FF ** -0.5, 0.21875, ((0, 8), (2, 4)))
    cotangent = noise(key_of[11], (WINDOW_TOKENS, D), 1.0, 6.0, ((0, 8),))
    return dict(resid=resid, queries=queries, rotated_key_value_pairs=rotated_key_value_pairs, doc_ids=doc_ids, out_weight=out_weight, norm_gain=norm_gain, routes=routes, probs=probs, w_gate=w_gate, w_up=w_up, w_down=w_down, cotangent=cotangent)


def reference(resid, queries, rotated_key_value_pairs, doc_ids, out_weight, norm_gain, routes, probs, w_gate, w_up, w_down, cotangent):
    group_width = QUERY_HEADS // KEY_VALUE_HEADS
    q_heads = queries.reshape(WINDOW_TOKENS, QUERY_HEADS, HEAD_DIMENSION)
    key_head_count = rotated_key_value_pairs[0].reshape(WINDOW_TOKENS, KEY_VALUE_HEADS, HEAD_DIMENSION)
    value_head_count = rotated_key_value_pairs[1].reshape(WINDOW_TOKENS, KEY_VALUE_HEADS, HEAD_DIMENSION)
    doc_row = doc_ids[0]
    positions = jnp.arange(WINDOW_TOKENS, dtype=jnp.int32)
    block_rows = min(512, WINDOW_TOKENS)
    block_count = WINDOW_TOKENS // block_rows
    score_scale = HEAD_DIMENSION ** (-0.5)

    def one_head(head_id):
        queries_h = jnp.take(q_heads, head_id, axis=1)
        keys_h = jnp.take(key_head_count, head_id // group_width, axis=1)
        values_h = jnp.take(value_head_count, head_id // group_width, axis=1)

        def one_block(block_id):
            first_row = block_id * block_rows
            query_rows = lax.dynamic_slice_in_dim(queries_h, first_row, block_rows, 0)
            query_pos = first_row + jnp.arange(block_rows, dtype=jnp.int32)
            query_doc = lax.dynamic_slice_in_dim(doc_row, first_row, block_rows, 0)
            scores = jnp.dot(query_rows, keys_h.T, preferred_element_type=jnp.float32) * score_scale
            visible = (positions[None, :] <= query_pos[:, None]) & (doc_row[None, :] == query_doc[:, None])
            scores = jnp.where(visible, scores, -1e+30)
            row_max = lax.optimization_barrier(jnp.max(scores, axis=-1, keepdims=True))
            weights = jnp.where(visible, jnp.exp(scores - row_max), 0.0)
            row_total = lax.optimization_barrier(jnp.sum(weights, axis=-1))
            mixed = jnp.dot(weights.astype(jnp.bfloat16), values_h, preferred_element_type=jnp.float32)
            return (mixed / row_total[:, None]).astype(jnp.bfloat16)
        return lax.map(one_block, jnp.arange(block_count, dtype=jnp.int32)).reshape(WINDOW_TOKENS, HEAD_DIMENSION)
    attn = lax.map(one_head, jnp.arange(QUERY_HEADS, dtype=jnp.int32))
    attn = jnp.transpose(attn, (1, 0, 2)).reshape(WINDOW_TOKENS, QUERY_HEADS * HEAD_DIMENSION)
    projected = jnp.dot(attn, out_weight, preferred_element_type=jnp.float32)
    hidden_state = (resid.astype(jnp.float32) + projected).astype(jnp.bfloat16)
    hstate = hidden_state.astype(jnp.float32)
    inverse = lax.rsqrt(lax.optimization_barrier(jnp.mean(hstate * hstate, axis=-1, keepdims=True)) + 1e-06)
    normed = (hstate * inverse * norm_gain).astype(jnp.bfloat16)
    flat_routes = routes.reshape(-1)
    assigned = WINDOW_TOKENS * TOPK
    per_block = TOK_DEV * TOPK
    block_total = WINDOW_TOKENS // TOK_DEV
    onehot = (flat_routes.reshape(block_total, per_block, 1) == jnp.arange(EXPERTS, dtype=jnp.int32)[None, None, :]).astype(jnp.int32)
    slot_rank = lax.optimization_barrier(jnp.sum((jnp.cumsum(onehot, axis=1) - onehot) * onehot, axis=2)).reshape(-1)
    block_of = jnp.arange(assigned, dtype=jnp.int32) // per_block
    slot_index = (flat_routes * block_total + block_of) * CAP + slot_rank
    slot_owner = jnp.full((EXPERTS * block_total * CAP,), assigned, jnp.int32)
    slot_owner = slot_owner.at[slot_index].set(jnp.arange(assigned, dtype=jnp.int32))
    slot_owner = slot_owner.reshape(EXPERTS, block_total * CAP)
    normed_pad = jnp.concatenate([normed, jnp.zeros((1, D), jnp.bfloat16)], axis=0)
    cot_pad = jnp.concatenate([cotangent, jnp.zeros((1, D), jnp.bfloat16)], axis=0)
    probs_pad = jnp.concatenate([probs.reshape(-1), jnp.zeros((1,), jnp.float32)])

    def one_expert(accum, inputs):
        owner_rows, gate_w, up_w, down_w = inputs
        token_rows = owner_rows // TOPK
        slot_inputs = normed_pad[token_rows]
        slot_probs = probs_pad[owner_rows]
        slot_grads = (slot_probs[:, None] * cot_pad[token_rows].astype(jnp.float32)).astype(jnp.bfloat16)
        gate_act = jnp.dot(slot_inputs, gate_w.T, preferred_element_type=jnp.float32)
        up_act = jnp.dot(slot_inputs, up_w.T, preferred_element_type=jnp.float32)
        sigma = jax.nn.sigmoid(gate_act)
        silu_gate = gate_act * sigma
        hidden = (silu_gate * up_act).astype(jnp.bfloat16)
        rounded_out = lax.optimization_barrier(jnp.dot(hidden, down_w, preferred_element_type=jnp.float32).astype(jnp.bfloat16))
        expert_out = rounded_out.astype(jnp.float32)
        accum = accum.at[token_rows].add(slot_probs[:, None] * expert_out, mode='drop')
        hidden_grad = jnp.dot(slot_grads, down_w.T, preferred_element_type=jnp.float32)
        gate_grad = (hidden_grad * up_act * sigma * (1.0 + gate_act * (1.0 - sigma))).astype(jnp.bfloat16)
        up_grad = (hidden_grad * silu_gate).astype(jnp.bfloat16)
        down_out = jnp.dot(hidden.T, slot_grads, preferred_element_type=jnp.float32).astype(jnp.bfloat16)
        gate_out = jnp.dot(gate_grad.T, slot_inputs, preferred_element_type=jnp.float32).astype(jnp.bfloat16)
        up_out = jnp.dot(up_grad.T, slot_inputs, preferred_element_type=jnp.float32).astype(jnp.bfloat16)
        return (accum, (gate_out, up_out, down_out))
    accum, grads = lax.scan(one_expert, jnp.zeros((WINDOW_TOKENS, D), jnp.float32), (slot_owner, w_gate, w_up, w_down))
    layer_out = (hstate + accum).astype(jnp.bfloat16)
    return (layer_out, grads[0], grads[1], grads[2])
```

```python
import functools
import math

import jax
import jax.numpy as jnp
from jax import lax
from jax.experimental import pallas as pl
from jax.experimental.pallas import tpu as pltpu
from jax.sharding import PartitionSpec as P

MESH = pl.DeviceIdType.MESH
BF16 = jnp.bfloat16
F32 = jnp.float32

HEAD_DIMENSION = 128


def attend_block(
    query_block, key_rows, value_rows, query_doc, key_doc, query_pos, key_pos, score_scale
):
    scores = (
        jnp.einsum("tgrd,sgd->gtrs", query_block, key_rows, preferred_element_type=jnp.float32)
        * score_scale
    )
    visible = (key_pos[None, :] <= query_pos[:, None]) & (key_doc[None, :] == query_doc[:, None])
    visible = visible[None, :, None, :]
    scores = jnp.where(visible, scores, -1e30)
    row_max = jnp.max(scores, axis=-1, keepdims=True)
    weights = jnp.where(visible, jnp.exp(scores - row_max), 0.0)
    row_total = jnp.sum(weights, axis=-1)
    mixed = jnp.einsum(
        "gtrs,sgd->tgrd",
        weights.astype(jnp.bfloat16),
        value_rows,
        preferred_element_type=jnp.float32,
    )
    return (mixed / jnp.transpose(row_total, (1, 0, 2))[..., None]).astype(jnp.bfloat16)


def forward_share(gate_share, up_share):
    sigma = jax.nn.sigmoid(gate_share)
    silu_gate = gate_share * sigma
    return (sigma, silu_gate, (silu_gate * up_share).astype(jnp.bfloat16))


def backward_share(grad_share, gate_share, up_share, sigma, silu_gate):
    gate_grad = (grad_share * up_share * sigma * (1.0 + gate_share * (1.0 - sigma))).astype(
        jnp.bfloat16
    )
    up_grad = (grad_share * silu_gate).astype(jnp.bfloat16)
    return (gate_grad, up_grad)


def per_device_slots(
    resid,
    queries,
    rotated_key_value_pairs,
    doc_ids,
    out_weight,
    norm_gain,
    routes,
    probs,
    w_gate,
    w_up,
    w_down,
    cotangent,
):
    tok_rows, model_width = resid.shape
    top_count = routes.shape[1]
    exp_dev = w_gate.shape[0]
    n_ctx = lax.axis_size("ctx")
    n_exp = lax.axis_size("exp")
    n_head = lax.axis_size("head")
    owners = n_ctx * n_exp
    experts = exp_dev * owners
    capacity = max(2, tok_rows * top_count * 5 // (4 * experts))
    head_size = HEAD_DIMENSION
    kv_local = rotated_key_value_pairs.shape[2] // head_size
    group_width = queries.shape[1] // (head_size * kv_local)
    whole_kv, whole_doc = (
        lax.all_gather(rotated_key_value_pairs, ("ctx", "exp"), axis=1, tiled=True),
        lax.all_gather(doc_ids, ("ctx", "exp"), axis=1, tiled=True),
    )
    total_rows = whole_kv.shape[1]
    key_rows = whole_kv[0].reshape(total_rows, kv_local, head_size)
    value_rows = whole_kv[1].reshape(total_rows, kv_local, head_size)
    key_doc = whole_doc[0]
    key_pos = jnp.arange(total_rows, dtype=jnp.int32)
    query_pos = lax.axis_index(("ctx", "exp")) * tok_rows + jnp.arange(tok_rows, dtype=jnp.int32)
    query_doc = doc_ids[0]
    group_step = math.gcd(group_width, max(1, 512 // tok_rows))
    block_count = group_width // group_step
    query_blocks = jnp.moveaxis(
        queries.reshape(tok_rows, kv_local, block_count, group_step, head_size), 2, 0
    )
    score_scale = head_size ** (-0.5)

    def attend_one(query_block):
        return attend_block(
            query_block, key_rows, value_rows, query_doc, key_doc, query_pos, key_pos, score_scale
        )

    attn = lax.map(attend_one, query_blocks)
    attn = jnp.moveaxis(attn, 0, 2).reshape(tok_rows, -1)
    partial_value = jnp.dot(
        attn,
        lax.all_gather(out_weight, ("ctx", "exp"), axis=1, tiled=True),
        preferred_element_type=jnp.float32,
    )
    attn_sum = lax.psum(partial_value, "head")
    hidden_state = (resid.astype(jnp.float32) + attn_sum).astype(jnp.bfloat16)
    hstate = hidden_state.astype(jnp.float32)
    inverse = lax.rsqrt(jnp.mean(hstate * hstate, axis=-1, keepdims=True) + 1e-06)
    normed = (hstate * inverse * norm_gain).astype(jnp.bfloat16)
    flat_routes = routes.reshape(-1)
    assigned = flat_routes.shape[0]
    onehot = (flat_routes[:, None] == jnp.arange(experts, dtype=jnp.int32)[None, :]).astype(
        jnp.int32
    )
    slot_rank = jnp.sum((jnp.cumsum(onehot, axis=0) - onehot) * onehot, axis=1)
    slot_index = flat_routes * capacity + slot_rank
    slot_owner = jnp.full((experts * capacity,), assigned, jnp.int32)
    slot_owner = slot_owner.at[slot_index].set(jnp.arange(assigned, dtype=jnp.int32))
    slot_rows = slot_owner // top_count
    flat_probs = probs.reshape(-1)
    probs_pad = jnp.concatenate([flat_probs, jnp.zeros((1,), jnp.float32)])
    head_index = lax.axis_index("head")
    quarter = model_width // n_head
    source_rows = lax.dynamic_slice_in_dim(normed, head_index * quarter, quarter, 1)
    source_cot = lax.dynamic_slice_in_dim(cotangent, head_index * quarter, quarter, 1)
    rows_pad = jnp.concatenate([source_rows, jnp.zeros((1, quarter), jnp.bfloat16)], axis=0)
    cot_pad = jnp.concatenate([source_cot, jnp.zeros((1, quarter), jnp.bfloat16)], axis=0)
    send_rows = rows_pad[slot_rows].reshape(owners, exp_dev * capacity, quarter)
    send_grads = (probs_pad[slot_owner][:, None] * cot_pad[slot_rows].astype(jnp.float32)).astype(
        jnp.bfloat16
    )
    send_grads = send_grads.reshape(owners, exp_dev * capacity, quarter)
    got_rows, got_grads = (
        lax.all_to_all(
            lax.all_to_all(
                send_rows.reshape(n_ctx, n_exp, exp_dev * capacity, quarter),
                "ctx",
                split_axis=0,
                concat_axis=0,
                tiled=True,
            ),
            "exp",
            split_axis=1,
            concat_axis=1,
            tiled=True,
        ),
        lax.all_to_all(
            lax.all_to_all(
                send_grads.reshape(n_ctx, n_exp, exp_dev * capacity, quarter),
                "ctx",
                split_axis=0,
                concat_axis=0,
                tiled=True,
            ),
            "exp",
            split_axis=1,
            concat_axis=1,
            tiled=True,
        ),
    )
    slot_inputs = got_rows.reshape(owners, exp_dev, capacity, quarter)
    slot_grads = got_grads.reshape(owners, exp_dev, capacity, quarter)
    gate_part = jnp.einsum(
        "secd,efd->secf", slot_inputs, w_gate, preferred_element_type=jnp.float32
    )
    up_part = jnp.einsum("secd,efd->secf", slot_inputs, w_up, preferred_element_type=jnp.float32)
    grad_part = jnp.einsum("secd,efd->secf", slot_grads, w_down, preferred_element_type=jnp.float32)
    gate_share, up_share = (
        lax.psum_scatter(gate_part, "head", scatter_dimension=3, tiled=True),
        lax.psum_scatter(up_part, "head", scatter_dimension=3, tiled=True),
    )
    sigma, silu_gate, hidden_share = forward_share(gate_share, up_share)
    hidden = lax.all_gather(hidden_share, "head", axis=3, tiled=True)
    grad_share = lax.psum_scatter(grad_part, "head", scatter_dimension=3, tiled=True)
    gate_grad_share, up_grad_share = backward_share(
        grad_share, gate_share, up_share, sigma, silu_gate
    )
    gate_grad, up_grad = (
        lax.all_gather(gate_grad_share, "head", axis=3, tiled=True),
        lax.all_gather(up_grad_share, "head", axis=3, tiled=True),
    )
    expert_out = jnp.einsum(
        "secf,efd->secd", hidden, w_down, preferred_element_type=jnp.float32
    ).astype(jnp.bfloat16)
    grad_down = jnp.einsum(
        "secf,secd->efd", hidden, slot_grads, preferred_element_type=jnp.float32
    ).astype(jnp.bfloat16)
    grad_gate = jnp.einsum(
        "secf,secd->efd", gate_grad, slot_inputs, preferred_element_type=jnp.float32
    ).astype(jnp.bfloat16)
    grad_up = jnp.einsum(
        "secf,secd->efd", up_grad, slot_inputs, preferred_element_type=jnp.float32
    ).astype(jnp.bfloat16)
    returned = lax.all_to_all(
        expert_out.reshape(owners, exp_dev * capacity, quarter),
        ("ctx", "exp"),
        split_axis=0,
        concat_axis=0,
        tiled=True,
    )
    returned = returned.reshape(experts * capacity, quarter)
    picked = returned[slot_index].astype(jnp.float32) * flat_probs[:, None]
    moe_part = jnp.sum(picked.reshape(tok_rows, top_count, quarter), axis=1)
    own_state = lax.dynamic_slice_in_dim(hstate, head_index * quarter, quarter, 1)
    layer_out = (own_state + moe_part).astype(jnp.bfloat16)
    return (layer_out, grad_gate, grad_up, grad_down)


def ring_id(ctx, head, exp):
    return {"ctx": ctx, "head": head, "exp": exp}


def remote(src, dst, send_sem, recv_sem, device):
    return pltpu.make_async_remote_copy(
        src_ref=src,
        dst_ref=dst,
        send_sem=send_sem,
        recv_sem=recv_sem,
        device_id=device,
        device_id_type=MESH,
    )


def greet(devices):
    barrier = pltpu.get_barrier_semaphore()
    for device in devices:
        pl.semaphore_signal(barrier, inc=1, device_id=device, device_id_type=MESH)
    pl.semaphore_wait(barrier, len(devices))


def token_group(n_exp):
    ctx, head, exp = lax.axis_index("ctx"), lax.axis_index("head"), lax.axis_index("exp")
    others = []
    for dx in range(2):
        for dz in range(n_exp):
            if dx or dz:
                to_ctx = 1 - ctx if dx else ctx
                to_exp = lax.rem(exp + dz, n_exp)
                from_exp = lax.rem(exp + n_exp - dz, n_exp)
                others.append(
                    (dx * n_exp + dz, ring_id(to_ctx, head, to_exp), to_ctx * n_exp + to_exp,
                     to_ctx * n_exp + from_exp)
                )
    return others


class Gather:
    def __init__(self, n_exp, own, block, send_sem, recv_sem):
        self.n_exp, self.own, self.block = n_exp, own, block
        self.send_sem, self.recv_sem = send_sem, recv_sem
        self.ctx, self.head = lax.axis_index("ctx"), lax.axis_index("head")
        self.exp = lax.axis_index("exp")
        self.me = self.ctx * n_exp + self.exp
        self.across = ring_id(1 - self.ctx, self.head, self.exp)
        self.sent = []

    def start(self):
        for dz in range(1, self.n_exp):
            device = ring_id(self.ctx, self.head, lax.rem(self.exp + dz, self.n_exp))
            self.send(self.own, self.me, dz, device)
        self.send(self.own, self.me, self.n_exp, self.across)

    def send(self, source, index, sem, device):
        copy = remote(
            source, self.block(index), self.send_sem.at[sem], self.recv_sem.at[sem], device
        )
        copy.start()
        self.sent.append(copy)

    def arrived(self, index, sem):
        remote(
            self.block(index),
            self.block(index),
            self.send_sem.at[sem],
            self.recv_sem.at[sem],
            self.across,
        ).wait_recv()

    def forward(self):
        for dz in range(1, self.n_exp):
            index = self.ctx * self.n_exp + lax.rem(self.exp + self.n_exp - dz, self.n_exp)
            self.arrived(index, dz)
            self.send(self.block(index), index, self.n_exp + dz, self.across)

    def finish(self):
        other = (1 - self.ctx) * self.n_exp
        self.arrived(other + self.exp, self.n_exp)
        for dz in range(1, self.n_exp):
            self.arrived(
                other + lax.rem(self.exp + self.n_exp - dz, self.n_exp), self.n_exp + dz
            )
        for copy in self.sent:
            copy.wait_send()


def attention_kernel(
    n_exp,
    heads,
    kv_ref,
    query_ref,
    doc_ref,
    meta_ref,
    cot_ref,
    attn_ref,
    cot_all,
    meta_all,
    kv_all,
    meta_send,
    meta_recv,
    kv_send,
    kv_recv,
    cot_send,
    cot_recv,
):
    rows, quarter = cot_all.shape[1:]
    me = lax.axis_index("ctx") * n_exp + lax.axis_index("exp")
    others = token_group(n_exp)
    greet([device for _, device, _, _ in others])

    def kv_block(index):
        return kv_all.at[:, pl.ds(pl.multiple_of(index * rows, rows), rows), :]

    kv_gather = Gather(n_exp, kv_ref, kv_block, kv_send, kv_recv)
    kv_gather.start()
    meta_copies = []
    for sem, device, to_block, _ in others:
        copy = remote(
            meta_ref.at[to_block], meta_all.at[me], meta_send.at[sem], meta_recv.at[sem], device
        )
        copy.start()
        meta_copies.append(copy)
    kv_all[:, pl.ds(pl.multiple_of(me * rows, rows), rows), :] = kv_ref[...]
    meta_all[me] = meta_ref[me]
    column = pl.multiple_of(lax.axis_index("head") * quarter, quarter)
    own_cot = cot_ref.at[:, pl.ds(column, quarter)]
    kv_gather.forward()
    cot_gather = Gather(n_exp, own_cot, lambda index: cot_all.at[index], cot_send, cot_recv)
    cot_gather.start()
    cot_all[me] = cot_ref[:, pl.ds(column, quarter)]
    kv_gather.finish()
    for sem, device, _, from_block in others:
        remote(
            meta_all.at[from_block],
            meta_all.at[from_block],
            meta_send.at[sem],
            meta_recv.at[sem],
            device,
        ).wait_recv()
    for copy in meta_copies:
        copy.wait_send()

    total = kv_all.shape[1]
    key_doc = jnp.concatenate([meta_all[s, 2:3, :] for s in range(total // rows)], axis=1)
    key_pos = lax.broadcasted_iota(jnp.int32, (rows, total), 1)
    query_pos = me * rows + lax.broadcasted_iota(jnp.int32, (rows, total), 0)
    visible = (key_pos <= query_pos) & (key_doc == doc_ref[:, 0:1])
    scale = HEAD_DIMENSION ** (-0.5)
    for head in range(heads):
        lanes = slice(head * HEAD_DIMENSION, (head + 1) * HEAD_DIMENSION)
        scores = lax.dot_general(
            query_ref[:, lanes], kv_all[0], (((1,), (1,)), ((), ())), preferred_element_type=F32
        )
        scores = jnp.where(visible, scores * scale, -1e30)
        weights = jnp.exp(scores - jnp.max(scores, axis=1, keepdims=True))
        row_total = jnp.sum(weights, axis=1, keepdims=True)
        mixed = jnp.dot(weights.astype(BF16), kv_all[1], preferred_element_type=F32)
        attn_ref[:, lanes] = (mixed / row_total).astype(BF16)
        if head == heads // 2:
            cot_gather.forward()
    cot_gather.finish()


def norm_kernel(
    n_exp,
    attn_ref,
    weight_ref,
    resid_ref,
    gain_ref,
    state_ref,
    normed_all,
    part_out,
    part_in,
    square_out,
    square_in,
    own_normed,
    part_send,
    part_recv,
    square_send,
    square_recv,
    token_send,
    token_recv,
):
    ctx, head, exp = lax.axis_index("ctx"), lax.axis_index("head"), lax.axis_index("exp")
    me = ctx * n_exp + exp
    rows, quarter = state_ref.shape
    width = resid_ref.shape[1]
    peers = {r: ring_id(ctx, head ^ r, exp) for r in (1, 2, 3)}
    along = [ring_id(ctx, head, lax.rem(exp + dz, n_exp)) for dz in range(1, n_exp)]
    greet([peers[r] for r in (1, 2, 3)] + along + [ring_id(1 - ctx, head, exp)])

    def partial(index):
        columns = pl.ds(pl.multiple_of(index * quarter, quarter), quarter)
        return jnp.dot(attn_ref[...], weight_ref[:, columns], preferred_element_type=F32)

    copies = []
    for r in (2, 3, 1):
        part_out[r - 1] = partial(head ^ r).astype(BF16)
        copy = remote(
            part_out.at[r - 1],
            part_in.at[r - 1],
            part_send.at[r - 1],
            part_recv.at[r - 1],
            peers[r],
        )
        copy.start()
        copies.append(copy)
    columns = pl.ds(pl.multiple_of(head * quarter, quarter), quarter)
    state = partial(head)
    for copy in copies:
        copy.wait_recv()
    for r in range(3):
        state = state + part_in[r].astype(F32)
    state = (resid_ref[:, columns].astype(F32) + state).astype(BF16)
    state_ref[...] = state
    state = state.astype(F32)
    squares = jnp.sum(state * state, axis=1, keepdims=True)
    square_out[...] = jnp.broadcast_to(squares, square_out.shape)
    square_copies = []
    for r in (2, 3, 1):
        copy = remote(
            square_out,
            square_in.at[r - 1],
            square_send.at[r - 1],
            square_recv.at[r - 1],
            peers[r],
        )
        copy.start()
        square_copies.append(copy)
    for copy in square_copies:
        copy.wait_recv()
    for r in range(3):
        squares = squares + square_in[r][:, 0:1]
    inverse = lax.rsqrt(squares / width + 1e-06)
    normed = (state * inverse * gain_ref[:, columns]).astype(BF16)
    own_normed[...] = normed
    gather = Gather(
        n_exp, own_normed, lambda index: normed_all.at[index], token_send, token_recv
    )
    gather.start()
    normed_all[me] = normed
    gather.forward()
    gather.finish()
    for copy in copies + square_copies:
        copy.wait_send()


def expert_kernel(
    n_exp,
    capacity,
    normed_ref,
    cot_ref,
    meta_ref,
    state_ref,
    gate_ref,
    up_ref,
    down_ref,
    layer_ref,
    grad_gate_ref,
    grad_up_ref,
    grad_down_ref,
    slot_in,
    slot_grad,
    picks,
    slot_prob,
    core_out,
    core_in,
    side_out,
    side_in,
    own_sum,
    acts,
    scaled,
    back_out,
    back_in,
    core_send,
    core_recv,
    side_send,
    side_recv,
    act_send,
    act_recv,
    back_send,
    back_recv,
):
    ctx, head, exp = lax.axis_index("ctx"), lax.axis_index("head"), lax.axis_index("exp")
    me = ctx * n_exp + exp
    blocks, rows, quarter = normed_ref.shape
    experts, hidden_units = gate_ref.shape[:2]
    share = blocks * capacity // 4
    core_peer, side_peer = ring_id(ctx, head ^ 1, exp), ring_id(ctx, head ^ 2, exp)
    others = token_group(n_exp)
    greet([core_peer, side_peer] + [device for _, device, _, _ in others])

    def place(e, s):
        return pl.ds(pl.multiple_of((e * blocks + s) * capacity, 16), capacity)

    for e in range(experts):

        @pl.loop(0, blocks)
        def _(s):
            meta = meta_ref[s]
            weight, rank = meta[e : e + 1, :], meta[4 + e : 5 + e, :]
            slot = lax.broadcasted_iota(jnp.int32, (capacity, rows), 0).astype(F32)
            pick = jnp.where((slot == rank) & (weight > 0.0), 1.0, 0.0)
            prob = jnp.sum(pick * weight, axis=1, keepdims=True)
            pick = pick.astype(BF16)
            picks[e * blocks + s] = pick
            slot_prob[place(e, s), :] = jnp.broadcast_to(prob, (capacity, 128))
            slot_in[place(e, s), :] = jnp.dot(
                pick, normed_ref[s], preferred_element_type=F32
            ).astype(BF16)
            slot_grad[place(e, s), :] = (
                prob * jnp.dot(pick, cot_ref[s], preferred_element_type=F32)
            ).astype(BF16)

    kinds = ((slot_in, gate_ref), (slot_in, up_ref), (slot_grad, down_ref))
    sent = []

    def rows_of(e, index):
        return pl.ds(pl.multiple_of(e * 4 * share + index * share, 16), share)

    def own_rows(index):
        return pl.ds(pl.multiple_of(index * share, 16), share)

    def partial(kind, e, index):
        data, weight = kinds[kind]
        return lax.dot_general(
            data[rows_of(e, index), :],
            weight[e],
            (((1,), (1,)), ((), ())),
            preferred_element_type=F32,
        )

    def begin(copy):
        copy.start()
        sent.append(copy)

    def core_copy(kind, e):
        n = kind * experts + e
        return remote(
            core_out.at[n], core_in.at[n], core_send.at[n], core_recv.at[n], core_peer
        )

    def side_copy(kind, e):
        n = kind * experts + e
        return remote(
            side_out.at[n], side_in.at[n], side_send.at[n], side_recv.at[n], side_peer
        )

    def reduce_start(kind, e):
        n = kind * experts + e
        core_out[n, 1] = partial(kind, e, head ^ 3).astype(BF16)
        core_out[n, 0] = partial(kind, e, head ^ 1).astype(BF16)
        begin(core_copy(kind, e))
        crossing = partial(kind, e, head ^ 2)
        core_copy(kind, e).wait_recv()
        side_out[n] = (crossing + core_in[n, 1].astype(F32)).astype(BF16)
        begin(side_copy(kind, e))
        own_sum[n] = partial(kind, e, head) + core_in[n, 0].astype(F32)

    def reduced(kind, e):
        n = kind * experts + e
        side_copy(kind, e).wait_recv()
        return own_sum[n] + side_in[n].astype(F32)

    def act_copy(kind, e, index, way):
        n = kind * experts + e
        view = acts.at[n, own_rows(index), :]
        device = side_peer if way == 0 else core_peer
        return remote(view, view, act_send.at[n * 3 + way], act_recv.at[n * 3 + way], device)

    def spread(kind, e, value):
        acts[kind * experts + e, own_rows(head), :] = value
        begin(act_copy(kind, e, head, 0))
        begin(act_copy(kind, e, head, 1))

    def pass_on(kind, e):
        act_copy(kind, e, head ^ 2, 0).wait_recv()
        begin(act_copy(kind, e, head ^ 2, 2))

    def spread_done(kind, e):
        act_copy(kind, e, head ^ 1, 1).wait_recv()
        act_copy(kind, e, head ^ 3, 2).wait_recv()

    for e in range(experts):
        for kind in (0, 1):
            reduce_start(kind, e)
    for e in range(experts):
        gate, up = reduced(0, e), reduced(1, e)
        own_sum[e], own_sum[experts + e] = gate, up
        sigma = 1.0 / (1.0 + jnp.exp(-gate))
        spread(0, e, (gate * sigma * up).astype(BF16))
        reduce_start(2, e)

    def weight_grad(kind, e, out, data):
        n = kind * experts + e
        source = data[pl.ds(e * 4 * share, 4 * share), :]
        for first in range(0, hidden_units, 256):
            out[e, first : first + 256, :] = lax.dot_general(
                acts[n, :, first : first + 256],
                source,
                (((0,), (0,)), ((), ())),
                preferred_element_type=F32,
            ).astype(BF16)

    for e in range(experts):
        pass_on(0, e)
    for e in range(experts):
        grad = reduced(2, e)
        gate, up = own_sum[e], own_sum[experts + e]
        sigma = 1.0 / (1.0 + jnp.exp(-gate))
        spread(1, e, (grad * up * sigma * (1.0 + gate * (1.0 - sigma))).astype(BF16))
        spread(2, e, (grad * gate * sigma).astype(BF16))
    for e in range(experts):
        spread_done(0, e)
        for index in range(4):
            part = pl.ds(index * share, share)
            whole = pl.ds((e * 4 + index) * share, share)
            out = jnp.dot(acts[e, part, :], down_ref[e], preferred_element_type=F32)
            out = out.astype(BF16).astype(F32)
            scaled[whole, :] = (slot_prob[whole, 0:1] * out).astype(BF16)

    @pl.loop(0, blocks)
    def _(s):
        total = jnp.zeros((rows, quarter), F32)
        for e in range(experts):
            total = total + lax.dot_general(
                picks[e * blocks + s],
                scaled[place(e, s), :],
                (((0,), (0,)), ((), ())),
                preferred_element_type=F32,
            )
        back_out[s] = total.astype(BF16)

    for sem, device, to_block, _ in others:
        begin(
            remote(
                back_out.at[to_block],
                back_in.at[sem],
                back_send.at[sem],
                back_recv.at[sem],
                device,
            )
        )
    for e in range(experts):
        weight_grad(0, e, grad_down_ref, slot_grad)
    for e in range(experts):
        for kind, out in ((1, grad_gate_ref), (2, grad_up_ref)):
            pass_on(kind, e)
            spread_done(kind, e)
            weight_grad(kind, e, out, slot_in)
    total = state_ref[...].astype(F32) + back_out[me].astype(F32)
    for sem, device, to_block, _ in others:
        remote(
            back_out.at[to_block], back_in.at[sem], back_send.at[sem], back_recv.at[sem], device
        ).wait_recv()
        total = total + back_in[sem].astype(F32)
    layer_ref[...] = total.astype(BF16)
    for copy in sent:
        copy.wait_send()


def per_device(
    resid,
    queries,
    rotated_key_value_pairs,
    doc_ids,
    out_weight,
    norm_gain,
    routes,
    probs,
    w_gate,
    w_up,
    w_down,
    cotangent,
):
    rows, width = resid.shape
    n_ctx, n_exp, n_head = (lax.axis_size(name) for name in ("ctx", "exp", "head"))
    experts_here, hidden_units, quarter = w_gate.shape
    owners = n_ctx * n_exp
    experts = experts_here * owners
    capacity = rows * routes.shape[1] * 5 // (4 * experts)
    if (
        n_ctx != 2
        or n_head != 4
        or experts_here != 2
        or capacity % 16
        or capacity * experts_here < rows
        or rotated_key_value_pairs.shape[2] != HEAD_DIMENSION
    ):
        return per_device_slots(
            resid,
            queries,
            rotated_key_value_pairs,
            doc_ids,
            out_weight,
            norm_gain,
            routes,
            probs,
            w_gate,
            w_up,
            w_down,
            cotangent,
        )
    dma = pltpu.SemaphoreType.DMA
    vmem = pl.BlockSpec(memory_space=pltpu.VMEM)
    shape = jax.ShapeDtypeStruct

    def params(number, mib):
        return pltpu.CompilerParams(
            collective_id=number, has_side_effects=True, vmem_limit_bytes=mib << 20
        )

    full_weight = lax.all_gather(out_weight, ("ctx", "exp"), axis=1, tiled=True)
    named = routes[:, :, None] == jnp.arange(experts, dtype=jnp.int32)[None, None, :]
    share = jnp.sum(jnp.where(named, probs[:, :, None], 0.0), axis=1)
    mask = jnp.any(named, axis=1).astype(BF16)
    earlier = jnp.tril(jnp.ones((rows, rows), BF16), -1)
    rank = jnp.dot(earlier, mask, preferred_element_type=F32)
    doc = doc_ids.astype(F32)
    spare = jnp.zeros((owners, 2, rows), F32)
    meta = jnp.concatenate(
        [
            share.T.reshape(owners, 2, rows),
            jnp.broadcast_to(doc[None], (owners, 2, rows)),
            rank.T.reshape(owners, 2, rows),
            spare,
        ],
        axis=1,
    )
    doc_column = jnp.broadcast_to(doc.T, (rows, 128))
    heads = queries.shape[1] // HEAD_DIMENSION
    total = owners * rows
    attn, cot_all, meta_all = pl.pallas_call(
        functools.partial(attention_kernel, n_exp, heads),
        out_shape=(
            shape(queries.shape, BF16),
            shape((owners, rows, quarter), BF16),
            shape(meta.shape, F32),
        ),
        in_specs=[vmem] * 5,
        out_specs=(vmem,) * 3,
        scratch_shapes=[
            pltpu.VMEM((2, total, HEAD_DIMENSION), BF16),
            dma((owners,)),
            dma((owners,)),
        ]
        + [dma((2 * n_exp,))] * 4,
        compiler_params=params(1, 24),
    )(rotated_key_value_pairs, queries, doc_column, meta, cotangent)
    state, normed_all = pl.pallas_call(
        functools.partial(norm_kernel, n_exp),
        out_shape=(shape((rows, quarter), BF16), shape((owners, rows, quarter), BF16)),
        in_specs=[vmem] * 4,
        out_specs=(vmem,) * 2,
        scratch_shapes=[
            pltpu.VMEM((3, rows, quarter), BF16),
            pltpu.VMEM((3, rows, quarter), BF16),
            pltpu.VMEM((rows, 128), F32),
            pltpu.VMEM((3, rows, 128), F32),
            pltpu.VMEM((rows, quarter), BF16),
        ]
        + [dma((3,))] * 4
        + [dma((2 * n_exp,))] * 2,
        compiler_params=params(2, 24),
    )(attn, full_weight, resid, norm_gain.reshape(1, width))
    slots = experts_here * owners * capacity
    quarter_rows = owners * capacity // 4
    pairs = 3 * experts_here
    grad_shape = shape(w_gate.shape, BF16)
    return pl.pallas_call(
        functools.partial(expert_kernel, n_exp, capacity),
        out_shape=(shape((rows, quarter), BF16), grad_shape, grad_shape, grad_shape),
        in_specs=[vmem] * 7,
        out_specs=(vmem,) * 4,
        scratch_shapes=[
            pltpu.VMEM((slots, quarter), BF16),
            pltpu.VMEM((slots, quarter), BF16),
            pltpu.VMEM((experts_here * owners, capacity, rows), BF16),
            pltpu.VMEM((slots, 128), F32),
            pltpu.VMEM((pairs, 2, quarter_rows, hidden_units), BF16),
            pltpu.VMEM((pairs, 2, quarter_rows, hidden_units), BF16),
            pltpu.VMEM((pairs, quarter_rows, hidden_units), BF16),
            pltpu.VMEM((pairs, quarter_rows, hidden_units), BF16),
            pltpu.VMEM((pairs, quarter_rows, hidden_units), F32),
            pltpu.VMEM((pairs, 4 * quarter_rows, hidden_units), BF16),
            pltpu.VMEM((slots, quarter), BF16),
            pltpu.VMEM((owners, rows, quarter), BF16),
            pltpu.VMEM((owners, rows, quarter), BF16),
        ]
        + [dma((pairs,))] * 4
        + [dma((3 * pairs,))] * 2
        + [dma((owners,))] * 2,
        compiler_params=params(3, 56),
    )(normed_all, cot_all, meta_all, state, w_gate, w_up, w_down)


def solution(mesh):
    return jax.shard_map(
        per_device,
        mesh=mesh,
        in_specs=(
            P(("ctx", "exp"), None),
            P(("ctx", "exp"), "head"),
            P(None, ("ctx", "exp"), "head"),
            P(None, ("ctx", "exp")),
            P("head", ("ctx", "exp")),
            P(),
            P(("ctx", "exp"), None),
            P(("ctx", "exp"), None),
            P(("ctx", "exp"), None, "head"),
            P(("ctx", "exp"), None, "head"),
            P(("ctx", "exp"), None, "head"),
            P(("ctx", "exp"), None),
        ),
        out_specs=(
            P(("ctx", "exp"), "head"),
            P(("ctx", "exp"), None, "head"),
            P(("ctx", "exp"), None, "head"),
            P(("ctx", "exp"), None, "head"),
        ),
        check_vma=False,
    )
```

```python
import functools
import math

import jax
import jax.numpy as jnp
from jax import lax
from jax.experimental import pallas as pl
from jax.experimental.pallas import tpu as pltpu
from jax.sharding import PartitionSpec as P

MESH = pl.DeviceIdType.MESH
BF16 = jnp.bfloat16
F32 = jnp.float32

HEAD_DIMENSION = 128


def attend_block(
    query_block, key_rows, value_rows, query_doc, key_doc, query_pos, key_pos, score_scale
):
    scores = (
        jnp.einsum("tgrd,sgd->gtrs", query_block, key_rows, preferred_element_type=jnp.float32)
        * score_scale
    )
    visible = (key_pos[None, :] <= query_pos[:, None]) & (key_doc[None, :] == query_doc[:, None])
    visible = visible[None, :, None, :]
    scores = jnp.where(visible, scores, -1e30)
    row_max = jnp.max(scores, axis=-1, keepdims=True)
    weights = jnp.where(visible, jnp.exp(scores - row_max), 0.0)
    row_total = jnp.sum(weights, axis=-1)
    mixed = jnp.einsum(
        "gtrs,sgd->tgrd",
        weights.astype(jnp.bfloat16),
        value_rows,
        preferred_element_type=jnp.float32,
    )
    return (mixed / jnp.transpose(row_total, (1, 0, 2))[..., None]).astype(jnp.bfloat16)


def forward_share(gate_share, up_share):
    sigma = jax.nn.sigmoid(gate_share)
    silu_gate = gate_share * sigma
    return (sigma, silu_gate, (silu_gate * up_share).astype(jnp.bfloat16))


def backward_share(grad_share, gate_share, up_share, sigma, silu_gate):
    gate_grad = (grad_share * up_share * sigma * (1.0 + gate_share * (1.0 - sigma))).astype(
        jnp.bfloat16
    )
    up_grad = (grad_share * silu_gate).astype(jnp.bfloat16)
    return (gate_grad, up_grad)


def per_device_slots(
    resid,
    queries,
    rotated_key_value_pairs,
    doc_ids,
    out_weight,
    norm_gain,
    routes,
    probs,
    w_gate,
    w_up,
    w_down,
    cotangent,
):
    tok_rows, model_width = resid.shape
    top_count = routes.shape[1]
    exp_dev = w_gate.shape[0]
    n_ctx = lax.axis_size("ctx")
    n_exp = lax.axis_size("exp")
    n_head = lax.axis_size("head")
    owners = n_ctx * n_exp
    experts = exp_dev * owners
    capacity = max(2, tok_rows * top_count * 5 // (4 * experts))
    head_size = HEAD_DIMENSION
    kv_local = rotated_key_value_pairs.shape[2] // head_size
    group_width = queries.shape[1] // (head_size * kv_local)
    whole_kv, whole_doc = (
        lax.all_gather(rotated_key_value_pairs, ("ctx", "exp"), axis=1, tiled=True),
        lax.all_gather(doc_ids, ("ctx", "exp"), axis=1, tiled=True),
    )
    total_rows = whole_kv.shape[1]
    key_rows = whole_kv[0].reshape(total_rows, kv_local, head_size)
    value_rows = whole_kv[1].reshape(total_rows, kv_local, head_size)
    key_doc = whole_doc[0]
    key_pos = jnp.arange(total_rows, dtype=jnp.int32)
    query_pos = lax.axis_index(("ctx", "exp")) * tok_rows + jnp.arange(tok_rows, dtype=jnp.int32)
    query_doc = doc_ids[0]
    group_step = math.gcd(group_width, max(1, 512 // tok_rows))
    block_count = group_width // group_step
    query_blocks = jnp.moveaxis(
        queries.reshape(tok_rows, kv_local, block_count, group_step, head_size), 2, 0
    )
    score_scale = head_size ** (-0.5)

    def attend_one(query_block):
        return attend_block(
            query_block, key_rows, value_rows, query_doc, key_doc, query_pos, key_pos, score_scale
        )

    attn = lax.map(attend_one, query_blocks)
    attn = jnp.moveaxis(attn, 0, 2).reshape(tok_rows, -1)
    partial_value = jnp.dot(
        attn,
        lax.all_gather(out_weight, ("ctx", "exp"), axis=1, tiled=True),
        preferred_element_type=jnp.float32,
    )
    attn_sum = lax.psum(partial_value, "head")
    hidden_state = (resid.astype(jnp.float32) + attn_sum).astype(jnp.bfloat16)
    hstate = hidden_state.astype(jnp.float32)
    inverse = lax.rsqrt(jnp.mean(hstate * hstate, axis=-1, keepdims=True) + 1e-06)
    normed = (hstate * inverse * norm_gain).astype(jnp.bfloat16)
    flat_routes = routes.reshape(-1)
    assigned = flat_routes.shape[0]
    onehot = (flat_routes[:, None] == jnp.arange(experts, dtype=jnp.int32)[None, :]).astype(
        jnp.int32
    )
    slot_rank = jnp.sum((jnp.cumsum(onehot, axis=0) - onehot) * onehot, axis=1)
    slot_index = flat_routes * capacity + slot_rank
    slot_owner = jnp.full((experts * capacity,), assigned, jnp.int32)
    slot_owner = slot_owner.at[slot_index].set(jnp.arange(assigned, dtype=jnp.int32))
    slot_rows = slot_owner // top_count
    flat_probs = probs.reshape(-1)
    probs_pad = jnp.concatenate([flat_probs, jnp.zeros((1,), jnp.float32)])
    head_index = lax.axis_index("head")
    quarter = model_width // n_head
    source_rows = lax.dynamic_slice_in_dim(normed, head_index * quarter, quarter, 1)
    source_cot = lax.dynamic_slice_in_dim(cotangent, head_index * quarter, quarter, 1)
    rows_pad = jnp.concatenate([source_rows, jnp.zeros((1, quarter), jnp.bfloat16)], axis=0)
    cot_pad = jnp.concatenate([source_cot, jnp.zeros((1, quarter), jnp.bfloat16)], axis=0)
    send_rows = rows_pad[slot_rows].reshape(owners, exp_dev * capacity, quarter)
    send_grads = (probs_pad[slot_owner][:, None] * cot_pad[slot_rows].astype(jnp.float32)).astype(
        jnp.bfloat16
    )
    send_grads = send_grads.reshape(owners, exp_dev * capacity, quarter)
    got_rows, got_grads = (
        lax.all_to_all(
            lax.all_to_all(
                send_rows.reshape(n_ctx, n_exp, exp_dev * capacity, quarter),
                "ctx",
                split_axis=0,
                concat_axis=0,
                tiled=True,
            ),
            "exp",
            split_axis=1,
            concat_axis=1,
            tiled=True,
        ),
        lax.all_to_all(
            lax.all_to_all(
                send_grads.reshape(n_ctx, n_exp, exp_dev * capacity, quarter),
                "ctx",
                split_axis=0,
                concat_axis=0,
                tiled=True,
            ),
            "exp",
            split_axis=1,
            concat_axis=1,
            tiled=True,
        ),
    )
    slot_inputs = got_rows.reshape(owners, exp_dev, capacity, quarter)
    slot_grads = got_grads.reshape(owners, exp_dev, capacity, quarter)
    gate_part = jnp.einsum(
        "secd,efd->secf", slot_inputs, w_gate, preferred_element_type=jnp.float32
    )
    up_part = jnp.einsum("secd,efd->secf", slot_inputs, w_up, preferred_element_type=jnp.float32)
    grad_part = jnp.einsum("secd,efd->secf", slot_grads, w_down, preferred_element_type=jnp.float32)
    gate_share, up_share = (
        lax.psum_scatter(gate_part, "head", scatter_dimension=3, tiled=True),
        lax.psum_scatter(up_part, "head", scatter_dimension=3, tiled=True),
    )
    sigma, silu_gate, hidden_share = forward_share(gate_share, up_share)
    hidden = lax.all_gather(hidden_share, "head", axis=3, tiled=True)
    grad_share = lax.psum_scatter(grad_part, "head", scatter_dimension=3, tiled=True)
    gate_grad_share, up_grad_share = backward_share(
        grad_share, gate_share, up_share, sigma, silu_gate
    )
    gate_grad, up_grad = (
        lax.all_gather(gate_grad_share, "head", axis=3, tiled=True),
        lax.all_gather(up_grad_share, "head", axis=3, tiled=True),
    )
    expert_out = jnp.einsum(
        "secf,efd->secd", hidden, w_down, preferred_element_type=jnp.float32
    ).astype(jnp.bfloat16)
    grad_down = jnp.einsum(
        "secf,secd->efd", hidden, slot_grads, preferred_element_type=jnp.float32
    ).astype(jnp.bfloat16)
    grad_gate = jnp.einsum(
        "secf,secd->efd", gate_grad, slot_inputs, preferred_element_type=jnp.float32
    ).astype(jnp.bfloat16)
    grad_up = jnp.einsum(
        "secf,secd->efd", up_grad, slot_inputs, preferred_element_type=jnp.float32
    ).astype(jnp.bfloat16)
    returned = lax.all_to_all(
        expert_out.reshape(owners, exp_dev * capacity, quarter),
        ("ctx", "exp"),
        split_axis=0,
        concat_axis=0,
        tiled=True,
    )
    returned = returned.reshape(experts * capacity, quarter)
    picked = returned[slot_index].astype(jnp.float32) * flat_probs[:, None]
    moe_part = jnp.sum(picked.reshape(tok_rows, top_count, quarter), axis=1)
    own_state = lax.dynamic_slice_in_dim(hstate, head_index * quarter, quarter, 1)
    layer_out = (own_state + moe_part).astype(jnp.bfloat16)
    return (layer_out, grad_gate, grad_up, grad_down)


def ring_id(ctx, head, exp):
    return {"ctx": ctx, "head": head, "exp": exp}


def remote(src, dst, send_sem, recv_sem, device):
    return pltpu.make_async_remote_copy(
        src_ref=src,
        dst_ref=dst,
        send_sem=send_sem,
        recv_sem=recv_sem,
        device_id=device,
        device_id_type=MESH,
    )


def greet(devices):
    barrier = pltpu.get_barrier_semaphore()
    for device in devices:
        pl.semaphore_signal(barrier, inc=1, device_id=device, device_id_type=MESH)
    pl.semaphore_wait(barrier, len(devices))


def token_group(n_exp):
    ctx, head, exp = lax.axis_index("ctx"), lax.axis_index("head"), lax.axis_index("exp")
    others = []
    for dx in range(2):
        for dz in range(n_exp):
            if dx or dz:
                to_ctx = 1 - ctx if dx else ctx
                to_exp = lax.rem(exp + dz, n_exp)
                from_exp = lax.rem(exp + n_exp - dz, n_exp)
                others.append(
                    (dx * n_exp + dz, ring_id(to_ctx, head, to_exp), to_ctx * n_exp + to_exp,
                     to_ctx * n_exp + from_exp)
                )
    return others


class Gather:
    def __init__(self, n_exp, own, block, send_sem, recv_sem):
        self.n_exp, self.own, self.block = n_exp, own, block
        self.send_sem, self.recv_sem = send_sem, recv_sem
        self.ctx, self.head = lax.axis_index("ctx"), lax.axis_index("head")
        self.exp = lax.axis_index("exp")
        self.me = self.ctx * n_exp + self.exp
        self.across = ring_id(1 - self.ctx, self.head, self.exp)
        self.sent = []

    def start(self):
        for dz in range(1, self.n_exp):
            device = ring_id(self.ctx, self.head, lax.rem(self.exp + dz, self.n_exp))
            self.send(self.own, self.me, dz, device)
        self.send(self.own, self.me, self.n_exp, self.across)

    def send(self, source, index, sem, device):
        copy = remote(
            source, self.block(index), self.send_sem.at[sem], self.recv_sem.at[sem], device
        )
        copy.start()
        self.sent.append(copy)

    def arrived(self, index, sem):
        remote(
            self.block(index),
            self.block(index),
            self.send_sem.at[sem],
            self.recv_sem.at[sem],
            self.across,
        ).wait_recv()

    def forward(self):
        for dz in range(1, self.n_exp):
            index = self.ctx * self.n_exp + lax.rem(self.exp + self.n_exp - dz, self.n_exp)
            self.arrived(index, dz)
            self.send(self.block(index), index, self.n_exp + dz, self.across)

    def finish(self):
        other = (1 - self.ctx) * self.n_exp
        self.arrived(other + self.exp, self.n_exp)
        for dz in range(1, self.n_exp):
            self.arrived(
                other + lax.rem(self.exp + self.n_exp - dz, self.n_exp), self.n_exp + dz
            )


def layer_kernel(
    n_exp,
    capacity,
    kv_ref,
    query_ref,
    doc_ref,
    meta_ref,
    cot_ref,
    weight_ref,
    resid_ref,
    gain_ref,
    gate_ref,
    up_ref,
    down_ref,
    layer_ref,
    grad_gate_ref,
    grad_up_ref,
    grad_down_ref,
    kv_all,
    cot_all,
    meta_all,
    weight_all,
    attn_all,
    part_out,
    part_in,
    cols_out,
    cols_in,
    square_out,
    square_in,
    own_normed,
    normed_all,
    slot_in,
    slot_grad,
    picks,
    slot_prob,
    core_out,
    core_in,
    side_out,
    side_in,
    own_sum,
    acts,
    scaled,
    back_out,
    back_in,
    meta_send,
    meta_recv,
    kv_send,
    kv_recv,
    cot_send,
    cot_recv,
    weight_send,
    weight_recv,
    line_send,
    line_recv,
    part_send,
    part_recv,
    cols_send,
    cols_recv,
    square_send,
    square_recv,
    token_send,
    token_recv,
    core_send,
    core_recv,
    side_send,
    side_recv,
    act_send,
    act_recv,
    back_send,
    back_recv,
):
    ctx, head, exp = lax.axis_index("ctx"), lax.axis_index("head"), lax.axis_index("exp")
    me = ctx * n_exp + exp
    blocks, rows, quarter = normed_all.shape
    width = resid_ref.shape[1]
    experts, hidden_units = gate_ref.shape[:2]
    share = blocks * capacity // 4
    half = quarter // 2
    core_peer, side_peer = ring_id(ctx, head ^ 1, exp), ring_id(ctx, head ^ 2, exp)
    across = ring_id(1 - ctx, head, exp)
    others = token_group(n_exp)
    greet(
        [
            ring_id(ctx, head ^ r, lax.rem(exp + dz, n_exp))
            for r in range(4)
            for dz in range(n_exp)
            if r or dz
        ]
        + [ring_id(1 - ctx, head, lax.rem(exp + dz, n_exp)) for dz in range(n_exp)]
    )
    sent = []

    def begin(copy):
        copy.start()
        sent.append(copy)

    def kv_block(index):
        return kv_all.at[:, pl.ds(pl.multiple_of(index * rows, rows), rows), :]

    kv_gather = Gather(n_exp, kv_ref, kv_block, kv_send, kv_recv)
    kv_gather.start()
    for sem, device, to_block, _ in others:
        begin(
            remote(
                meta_ref.at[to_block], meta_all.at[me], meta_send.at[sem], meta_recv.at[sem], device
            )
        )
    kv_all[:, pl.ds(pl.multiple_of(me * rows, rows), rows), :] = kv_ref[...]
    meta_all[me] = meta_ref[me]
    kv_gather.forward()
    begin(
        remote(weight_ref, weight_all.at[ctx], weight_send.at[0], weight_recv.at[0], across)
    )
    weight_all[ctx] = weight_ref[...]
    columns = pl.ds(pl.multiple_of(head * quarter, quarter), quarter)
    cot_gather = Gather(
        n_exp, cot_ref.at[:, columns], lambda index: cot_all.at[index], cot_send, cot_recv
    )
    cot_gather.start()
    cot_all[me] = cot_ref[:, columns]
    for sem, device, _, from_block in others:
        remote(
            meta_all.at[from_block],
            meta_all.at[from_block],
            meta_send.at[sem],
            meta_recv.at[sem],
            device,
        ).wait_recv()
    kv_gather.finish()

    total = kv_all.shape[1]
    key_doc = jnp.concatenate([meta_all[s, 2:3, :] for s in range(total // rows)], axis=1)
    key_pos = lax.broadcasted_iota(jnp.int32, (rows, total), 1)
    query_pos = me * rows + lax.broadcasted_iota(jnp.int32, (rows, total), 0)
    visible = (key_pos <= query_pos) & (key_doc == doc_ref[:, 0:1])
    scale = HEAD_DIMENSION ** (-0.5)
    heads = query_ref.shape[1] // HEAD_DIMENSION
    chunks = 4
    chunk_lanes = query_ref.shape[1] // chunks

    def line_copy(way, c, k, receive):
        index = exp - k if way == 0 else exp + k
        view = attn_all.at[index, :, c * chunk_lanes : (c + 1) * chunk_lanes]
        first = (way * chunks + c) * n_exp
        device = ring_id(ctx, head, exp + 1 if way == 0 else exp - 1)
        if receive:
            device = across
        return remote(
            view,
            view,
            line_send.at[first + k],
            line_recv.at[first + (k if receive else k + 1)],
            device,
        )

    def holds(way, k):
        return exp >= k if way == 0 else exp <= n_exp - 1 - k

    def passes(way, k):
        return holds(way, k) & (exp < n_exp - 1 if way == 0 else exp > 0)

    def line_pass(c, k):
        for way in range(2):
            if k:

                @pl.when(holds(way, k))
                def _():
                    line_copy(way, c, k, True).wait_recv()

            if k < n_exp - 1:

                @pl.when(passes(way, k))
                def _():
                    line_copy(way, c, k, False).start()

    for c in range(chunks):
        for number in range(c * heads // chunks, (c + 1) * heads // chunks):
            lanes = slice(number * HEAD_DIMENSION, (number + 1) * HEAD_DIMENSION)
            scores = lax.dot_general(
                query_ref[:, lanes], kv_all[0], (((1,), (1,)), ((), ())), preferred_element_type=F32
            )
            scores = jnp.where(visible, scores * scale, -1e30)
            weights = jnp.exp(scores - jnp.max(scores, axis=1, keepdims=True))
            row_total = jnp.sum(weights, axis=1, keepdims=True)
            mixed = jnp.dot(weights.astype(BF16), kv_all[1], preferred_element_type=F32)
            attn_all[exp, :, lanes] = (mixed / row_total).astype(BF16)
        line_pass(c, 0)
        if c:
            line_pass(c - 1, 1)
        if c == 2:
            cot_gather.forward()
    line_pass(chunks - 1, 1)
    for c in range(chunks):
        line_pass(c, 2)

    def place(e, s):
        return pl.ds(pl.multiple_of((e * blocks + s) * capacity, 16), capacity)

    cot_gather.finish()
    for e in range(experts):

        @pl.loop(0, blocks)
        def _(s):
            meta = meta_all[s]
            weight, rank = meta[e : e + 1, :], meta[4 + e : 5 + e, :]
            slot = lax.broadcasted_iota(jnp.int32, (capacity, rows), 0).astype(F32)
            pick = jnp.where((slot == rank) & (weight > 0.0), 1.0, 0.0)
            prob = jnp.sum(pick * weight, axis=1, keepdims=True)
            pick = pick.astype(BF16)
            picks[e * blocks + s] = pick
            slot_prob[place(e, s), :] = jnp.broadcast_to(prob, (capacity, 128))
            slot_grad[place(e, s), :] = (
                prob * jnp.dot(pick, cot_all[s], preferred_element_type=F32)
            ).astype(BF16)

    for c in range(chunks):
        line_pass(c, 3)
    weight_view = weight_all.at[1 - ctx]
    remote(
        weight_view, weight_view, weight_send.at[0], weight_recv.at[0], across
    ).wait_recv()

    def projected(index):
        block = attn_all[index]
        return jnp.concatenate(
            [jnp.dot(block, weight_all[p], preferred_element_type=F32) for p in range(2)], axis=1
        )

    part_copies = []
    for r in (2, 3, 1):
        part_out[r - 1] = projected(head ^ r).astype(BF16)
        copy = remote(
            part_out.at[r - 1],
            part_in.at[r - 1],
            part_send.at[r - 1],
            part_recv.at[r - 1],
            ring_id(ctx, head ^ r, exp),
        )
        begin(copy)
        part_copies.append(copy)
    state = projected(head)
    for copy in part_copies:
        copy.wait_recv()
    for r in range(3):
        state = state + part_in[r].astype(F32)
    side = lax.rem(exp, 2)
    for p in range(2):
        cols_out[p] = state[:, p * half : (p + 1) * half].astype(BF16)

    def cols_copy(p):
        target = 2 * p + lax.div(exp, 2)
        own = (target == head) & (head == exp)
        copy = remote(
            cols_out.at[p],
            cols_in.at[side],
            cols_send.at[p],
            cols_recv.at[side],
            ring_id(ctx, target, head),
        )
        return own, copy

    for p in range(2):
        own, copy = cols_copy(p)

        @pl.when(jnp.logical_not(own))
        def _():
            copy.start()

        @pl.when(own)
        def _():
            cols_in[side] = cols_out[p]

    for p in range(2):
        source = 2 * lax.rem(head, 2) + p
        own = (source == exp) & (head == exp)

        @pl.when(jnp.logical_not(own))
        def _():
            view = cols_in.at[p]
            remote(view, view, cols_send.at[p], cols_recv.at[p], across).wait_recv()

    state = jnp.concatenate([cols_in[0], cols_in[1]], axis=1).astype(F32)
    state = (resid_ref[:, columns].astype(F32) + state).astype(BF16)
    layer_ref[...] = state
    state = state.astype(F32)
    squares = jnp.sum(state * state, axis=1, keepdims=True)
    square_out[...] = jnp.broadcast_to(squares, square_out.shape)
    square_copies = []
    for r in (2, 3, 1):
        copy = remote(
            square_out,
            square_in.at[r - 1],
            square_send.at[r - 1],
            square_recv.at[r - 1],
            ring_id(ctx, head ^ r, exp),
        )
        begin(copy)
        square_copies.append(copy)
    for copy in square_copies:
        copy.wait_recv()
    for r in range(3):
        squares = squares + square_in[r][:, 0:1]
    inverse = lax.rsqrt(squares / width + 1e-06)
    normed = (state * inverse * gain_ref[:, columns]).astype(BF16)
    own_normed[...] = normed
    token_gather = Gather(
        n_exp, own_normed, lambda index: normed_all.at[index], token_send, token_recv
    )
    token_gather.start()
    normed_all[me] = normed

    kinds = ((slot_in, gate_ref), (slot_in, up_ref), (slot_grad, down_ref))
    def rows_of(e, index):
        return pl.ds(pl.multiple_of(e * 4 * share + index * share, 16), share)

    def own_rows(index):
        return pl.ds(pl.multiple_of(index * share, 16), share)

    def partial(kind, e, index):
        data, weight = kinds[kind]
        return lax.dot_general(
            data[rows_of(e, index), :],
            weight[e],
            (((1,), (1,)), ((), ())),
            preferred_element_type=F32,
        )

    def core_copy(kind, e):
        n = kind * experts + e
        return remote(
            core_out.at[n], core_in.at[n], core_send.at[n], core_recv.at[n], core_peer
        )

    def side_copy(kind, e):
        n = kind * experts + e
        return remote(
            side_out.at[n], side_in.at[n], side_send.at[n], side_recv.at[n], side_peer
        )

    def reduce_start(kind, e):
        n = kind * experts + e
        core_out[n, 1] = partial(kind, e, head ^ 3).astype(BF16)
        core_out[n, 0] = partial(kind, e, head ^ 1).astype(BF16)
        begin(core_copy(kind, e))
        crossing = partial(kind, e, head ^ 2)
        core_copy(kind, e).wait_recv()
        side_out[n] = (crossing + core_in[n, 1].astype(F32)).astype(BF16)
        begin(side_copy(kind, e))
        own_sum[n] = partial(kind, e, head) + core_in[n, 0].astype(F32)

    def reduced(kind, e):
        n = kind * experts + e
        side_copy(kind, e).wait_recv()
        return own_sum[n] + side_in[n].astype(F32)

    def act_copy(kind, e, index, way):
        n = kind * experts + e
        view = acts.at[n, own_rows(index), :]
        device = side_peer if way == 0 else core_peer
        return remote(view, view, act_send.at[n * 3 + way], act_recv.at[n * 3 + way], device)

    def spread(kind, e, value):
        acts[kind * experts + e, own_rows(head), :] = value
        begin(act_copy(kind, e, head, 0))
        begin(act_copy(kind, e, head, 1))

    def pass_on(kind, e):
        act_copy(kind, e, head ^ 2, 0).wait_recv()
        begin(act_copy(kind, e, head ^ 2, 2))

    def spread_done(kind, e):
        act_copy(kind, e, head ^ 1, 1).wait_recv()
        act_copy(kind, e, head ^ 3, 2).wait_recv()

    reduce_start(2, 0)
    token_gather.forward()
    for e in range(1, experts):
        reduce_start(2, e)
    token_gather.finish()
    for e in range(experts):

        @pl.loop(0, blocks)
        def _(s):
            slot_in[place(e, s), :] = jnp.dot(
                picks[e * blocks + s], normed_all[s], preferred_element_type=F32
            ).astype(BF16)

        for kind in (0, 1):
            reduce_start(kind, e)
    for e in range(experts):
        gate, up = reduced(0, e), reduced(1, e)
        own_sum[e], own_sum[experts + e] = gate, up
        sigma = 1.0 / (1.0 + jnp.exp(-gate))
        spread(0, e, (gate * sigma * up).astype(BF16))

    def weight_grad(kind, e, out, data):
        n = kind * experts + e
        source = data[pl.ds(e * 4 * share, 4 * share), :]
        for first in range(0, hidden_units, 256):
            out[e, first : first + 256, :] = lax.dot_general(
                acts[n, :, first : first + 256],
                source,
                (((0,), (0,)), ((), ())),
                preferred_element_type=F32,
            ).astype(BF16)

    for e in range(experts):
        pass_on(0, e)
    for e in range(experts):
        grad = reduced(2, e)
        gate, up = own_sum[e], own_sum[experts + e]
        sigma = 1.0 / (1.0 + jnp.exp(-gate))
        spread(1, e, (grad * up * sigma * (1.0 + gate * (1.0 - sigma))).astype(BF16))
        spread(2, e, (grad * gate * sigma).astype(BF16))
    for e in range(experts):
        spread_done(0, e)
        for index in range(4):
            part = pl.ds(index * share, share)
            whole = pl.ds((e * 4 + index) * share, share)
            out = jnp.dot(acts[e, part, :], down_ref[e], preferred_element_type=F32)
            out = out.astype(BF16).astype(F32)
            scaled[whole, :] = (slot_prob[whole, 0:1] * out).astype(BF16)

    @pl.loop(0, blocks)
    def _(s):
        total = jnp.zeros((rows, quarter), F32)
        for e in range(experts):
            total = total + lax.dot_general(
                picks[e * blocks + s],
                scaled[place(e, s), :],
                (((0,), (0,)), ((), ())),
                preferred_element_type=F32,
            )
        back_out[s] = total.astype(BF16)

    for sem, device, to_block, _ in others:
        begin(
            remote(
                back_out.at[to_block],
                back_in.at[sem],
                back_send.at[sem],
                back_recv.at[sem],
                device,
            )
        )
    for e in range(experts):
        weight_grad(0, e, grad_down_ref, slot_grad)
    for e in range(experts):
        for kind, out in ((1, grad_gate_ref), (2, grad_up_ref)):
            pass_on(kind, e)
            spread_done(kind, e)
            weight_grad(kind, e, out, slot_in)
    total = layer_ref[...].astype(F32) + back_out[me].astype(F32)
    for sem, device, to_block, _ in others:
        remote(
            back_out.at[to_block], back_in.at[sem], back_send.at[sem], back_recv.at[sem], device
        ).wait_recv()
        total = total + back_in[sem].astype(F32)
    layer_ref[...] = total.astype(BF16)
    for copy in sent + kv_gather.sent + cot_gather.sent + token_gather.sent:
        copy.wait_send()
    for p in range(2):
        own, copy = cols_copy(p)

        @pl.when(jnp.logical_not(own))
        def _():
            copy.wait_send()

    for way in range(2):
        for c in range(chunks):
            for k in range(n_exp - 1):

                @pl.when(passes(way, k))
                def _():
                    line_copy(way, c, k, False).wait_send()


def per_device(
    resid,
    queries,
    rotated_key_value_pairs,
    doc_ids,
    out_weight,
    norm_gain,
    routes,
    probs,
    w_gate,
    w_up,
    w_down,
    cotangent,
):
    rows, width = resid.shape
    n_ctx, n_exp, n_head = (lax.axis_size(name) for name in ("ctx", "exp", "head"))
    experts_here, hidden_units, quarter = w_gate.shape
    owners = n_ctx * n_exp
    experts = experts_here * owners
    capacity = rows * routes.shape[1] * 5 // (4 * experts)
    if (
        n_ctx != 2
        or n_head != 4
        or n_exp != n_head
        or experts_here != 2
        or capacity % 16
        or capacity * experts_here < rows
        or rotated_key_value_pairs.shape[2] != HEAD_DIMENSION
    ):
        return per_device_slots(
            resid,
            queries,
            rotated_key_value_pairs,
            doc_ids,
            out_weight,
            norm_gain,
            routes,
            probs,
            w_gate,
            w_up,
            w_down,
            cotangent,
        )
    dma = pltpu.SemaphoreType.DMA
    vmem = pl.BlockSpec(memory_space=pltpu.VMEM)
    shape = jax.ShapeDtypeStruct

    named = routes[:, :, None] == jnp.arange(experts, dtype=jnp.int32)[None, None, :]
    share = jnp.sum(jnp.where(named, probs[:, :, None], 0.0), axis=1)
    mask = jnp.any(named, axis=1).astype(BF16)
    earlier = jnp.tril(jnp.ones((rows, rows), BF16), -1)
    rank = jnp.dot(earlier, mask, preferred_element_type=F32)
    doc = doc_ids.astype(F32)
    spare = jnp.zeros((owners, 2, rows), F32)
    meta = jnp.concatenate(
        [
            share.T.reshape(owners, 2, rows),
            jnp.broadcast_to(doc[None], (owners, 2, rows)),
            rank.T.reshape(owners, 2, rows),
            spare,
        ],
        axis=1,
    )
    doc_column = jnp.broadcast_to(doc.T, (rows, 128))
    total = owners * rows
    lanes = queries.shape[1]
    slots = experts_here * owners * capacity
    quarter_rows = owners * capacity // 4
    pairs = 3 * experts_here
    grad_shape = shape(w_gate.shape, BF16)
    return pl.pallas_call(
        functools.partial(layer_kernel, n_exp, capacity),
        out_shape=(shape((rows, quarter), BF16), grad_shape, grad_shape, grad_shape),
        in_specs=[vmem] * 11,
        out_specs=(vmem,) * 4,
        scratch_shapes=[
            pltpu.VMEM((2, total, HEAD_DIMENSION), BF16),
            pltpu.VMEM((owners, rows, quarter), BF16),
            pltpu.VMEM(meta.shape, F32),
            pltpu.VMEM((2, lanes, quarter // 2), BF16),
            pltpu.VMEM((n_exp, rows, lanes), BF16),
            pltpu.VMEM((3, rows, quarter), BF16),
            pltpu.VMEM((3, rows, quarter), BF16),
            pltpu.VMEM((2, rows, quarter // 2), BF16),
            pltpu.VMEM((2, rows, quarter // 2), BF16),
            pltpu.VMEM((rows, 128), F32),
            pltpu.VMEM((3, rows, 128), F32),
            pltpu.VMEM((rows, quarter), BF16),
            pltpu.VMEM((owners, rows, quarter), BF16),
            pltpu.VMEM((slots, quarter), BF16),
            pltpu.VMEM((slots, quarter), BF16),
            pltpu.VMEM((experts_here * owners, capacity, rows), BF16),
            pltpu.VMEM((slots, 128), F32),
            pltpu.VMEM((pairs, 2, quarter_rows, hidden_units), BF16),
            pltpu.VMEM((pairs, 2, quarter_rows, hidden_units), BF16),
            pltpu.VMEM((pairs, quarter_rows, hidden_units), BF16),
            pltpu.VMEM((pairs, quarter_rows, hidden_units), BF16),
            pltpu.VMEM((pairs, quarter_rows, hidden_units), F32),
            pltpu.VMEM((pairs, 4 * quarter_rows, hidden_units), BF16),
            pltpu.VMEM((slots, quarter), BF16),
            pltpu.VMEM((owners, rows, quarter), BF16),
            pltpu.VMEM((owners, rows, quarter), BF16),
            dma((owners,)),
            dma((owners,)),
        ]
        + [dma((2 * n_exp,))] * 4
        + [dma((1,))] * 2
        + [dma((8 * n_exp,))] * 2
        + [dma((3,))] * 2
        + [dma((2,))] * 2
        + [dma((3,))] * 2
        + [dma((2 * n_exp,))] * 2
        + [dma((pairs,))] * 4
        + [dma((3 * pairs,))] * 2
        + [dma((owners,))] * 2,
        compiler_params=pltpu.CompilerParams(
            collective_id=1, has_side_effects=True, vmem_limit_bytes=58 << 20
        ),
    )(
        rotated_key_value_pairs,
        queries,
        doc_column,
        meta,
        cotangent,
        out_weight,
        resid,
        norm_gain.reshape(1, width),
        w_gate,
        w_up,
        w_down,
    )


def solution(mesh):
    return jax.shard_map(
        per_device,
        mesh=mesh,
        in_specs=(
            P(("ctx", "exp"), None),
            P(("ctx", "exp"), "head"),
            P(None, ("ctx", "exp"), "head"),
            P(None, ("ctx", "exp")),
            P("head", ("ctx", "exp")),
            P(),
            P(("ctx", "exp"), None),
            P(("ctx", "exp"), None),
            P(("ctx", "exp"), None, "head"),
            P(("ctx", "exp"), None, "head"),
            P(("ctx", "exp"), None, "head"),
            P(("ctx", "exp"), None),
        ),
        out_specs=(
            P(("ctx", "exp"), "head"),
            P(("ctx", "exp"), None, "head"),
            P(("ctx", "exp"), None, "head"),
            P(("ctx", "exp"), None, "head"),
        ),
        check_vma=False,
    )
```

```python
import functools
import math

import jax
import jax.numpy as jnp
from jax import lax
from jax.experimental import pallas as pl
from jax.experimental.pallas import tpu as pltpu
from jax.sharding import PartitionSpec as P

MESH = pl.DeviceIdType.MESH
BF16 = jnp.bfloat16
F32 = jnp.float32

HEAD_DIMENSION = 128


def attend_block(
    query_block, key_rows, value_rows, query_doc, key_doc, query_pos, key_pos, score_scale
):
    scores = (
        jnp.einsum("tgrd,sgd->gtrs", query_block, key_rows, preferred_element_type=jnp.float32)
        * score_scale
    )
    visible = (key_pos[None, :] <= query_pos[:, None]) & (key_doc[None, :] == query_doc[:, None])
    visible = visible[None, :, None, :]
    scores = jnp.where(visible, scores, -1e30)
    row_max = jnp.max(scores, axis=-1, keepdims=True)
    weights = jnp.where(visible, jnp.exp(scores - row_max), 0.0)
    row_total = jnp.sum(weights, axis=-1)
    mixed = jnp.einsum(
        "gtrs,sgd->tgrd",
        weights.astype(jnp.bfloat16),
        value_rows,
        preferred_element_type=jnp.float32,
    )
    return (mixed / jnp.transpose(row_total, (1, 0, 2))[..., None]).astype(jnp.bfloat16)


def forward_share(gate_share, up_share):
    sigma = jax.nn.sigmoid(gate_share)
    silu_gate = gate_share * sigma
    return (sigma, silu_gate, (silu_gate * up_share).astype(jnp.bfloat16))


def backward_share(grad_share, gate_share, up_share, sigma, silu_gate):
    gate_grad = (grad_share * up_share * sigma * (1.0 + gate_share * (1.0 - sigma))).astype(
        jnp.bfloat16
    )
    up_grad = (grad_share * silu_gate).astype(jnp.bfloat16)
    return (gate_grad, up_grad)


def per_device_slots(
    resid,
    queries,
    rotated_key_value_pairs,
    doc_ids,
    out_weight,
    norm_gain,
    routes,
    probs,
    w_gate,
    w_up,
    w_down,
    cotangent,
):
    tok_rows, model_width = resid.shape
    top_count = routes.shape[1]
    exp_dev = w_gate.shape[0]
    n_ctx = lax.axis_size("ctx")
    n_exp = lax.axis_size("exp")
    n_head = lax.axis_size("head")
    owners = n_ctx * n_exp
    experts = exp_dev * owners
    capacity = max(2, tok_rows * top_count * 5 // (4 * experts))
    head_size = HEAD_DIMENSION
    kv_local = rotated_key_value_pairs.shape[2] // head_size
    group_width = queries.shape[1] // (head_size * kv_local)
    whole_kv, whole_doc = (
        lax.all_gather(rotated_key_value_pairs, ("ctx", "exp"), axis=1, tiled=True),
        lax.all_gather(doc_ids, ("ctx", "exp"), axis=1, tiled=True),
    )
    total_rows = whole_kv.shape[1]
    key_rows = whole_kv[0].reshape(total_rows, kv_local, head_size)
    value_rows = whole_kv[1].reshape(total_rows, kv_local, head_size)
    key_doc = whole_doc[0]
    key_pos = jnp.arange(total_rows, dtype=jnp.int32)
    query_pos = lax.axis_index(("ctx", "exp")) * tok_rows + jnp.arange(tok_rows, dtype=jnp.int32)
    query_doc = doc_ids[0]
    group_step = math.gcd(group_width, max(1, 512 // tok_rows))
    block_count = group_width // group_step
    query_blocks = jnp.moveaxis(
        queries.reshape(tok_rows, kv_local, block_count, group_step, head_size), 2, 0
    )
    score_scale = head_size ** (-0.5)

    def attend_one(query_block):
        return attend_block(
            query_block, key_rows, value_rows, query_doc, key_doc, query_pos, key_pos, score_scale
        )

    attn = lax.map(attend_one, query_blocks)
    attn = jnp.moveaxis(attn, 0, 2).reshape(tok_rows, -1)
    partial_value = jnp.dot(
        attn,
        lax.all_gather(out_weight, ("ctx", "exp"), axis=1, tiled=True),
        preferred_element_type=jnp.float32,
    )
    attn_sum = lax.psum(partial_value, "head")
    hidden_state = (resid.astype(jnp.float32) + attn_sum).astype(jnp.bfloat16)
    hstate = hidden_state.astype(jnp.float32)
    inverse = lax.rsqrt(jnp.mean(hstate * hstate, axis=-1, keepdims=True) + 1e-06)
    normed = (hstate * inverse * norm_gain).astype(jnp.bfloat16)
    flat_routes = routes.reshape(-1)
    assigned = flat_routes.shape[0]
    onehot = (flat_routes[:, None] == jnp.arange(experts, dtype=jnp.int32)[None, :]).astype(
        jnp.int32
    )
    slot_rank = jnp.sum((jnp.cumsum(onehot, axis=0) - onehot) * onehot, axis=1)
    slot_index = flat_routes * capacity + slot_rank
    slot_owner = jnp.full((experts * capacity,), assigned, jnp.int32)
    slot_owner = slot_owner.at[slot_index].set(jnp.arange(assigned, dtype=jnp.int32))
    slot_rows = slot_owner // top_count
    flat_probs = probs.reshape(-1)
    probs_pad = jnp.concatenate([flat_probs, jnp.zeros((1,), jnp.float32)])
    head_index = lax.axis_index("head")
    quarter = model_width // n_head
    source_rows = lax.dynamic_slice_in_dim(normed, head_index * quarter, quarter, 1)
    source_cot = lax.dynamic_slice_in_dim(cotangent, head_index * quarter, quarter, 1)
    rows_pad = jnp.concatenate([source_rows, jnp.zeros((1, quarter), jnp.bfloat16)], axis=0)
    cot_pad = jnp.concatenate([source_cot, jnp.zeros((1, quarter), jnp.bfloat16)], axis=0)
    send_rows = rows_pad[slot_rows].reshape(owners, exp_dev * capacity, quarter)
    send_grads = (probs_pad[slot_owner][:, None] * cot_pad[slot_rows].astype(jnp.float32)).astype(
        jnp.bfloat16
    )
    send_grads = send_grads.reshape(owners, exp_dev * capacity, quarter)
    got_rows, got_grads = (
        lax.all_to_all(
            lax.all_to_all(
                send_rows.reshape(n_ctx, n_exp, exp_dev * capacity, quarter),
                "ctx",
                split_axis=0,
                concat_axis=0,
                tiled=True,
            ),
            "exp",
            split_axis=1,
            concat_axis=1,
            tiled=True,
        ),
        lax.all_to_all(
            lax.all_to_all(
                send_grads.reshape(n_ctx, n_exp, exp_dev * capacity, quarter),
                "ctx",
                split_axis=0,
                concat_axis=0,
                tiled=True,
            ),
            "exp",
            split_axis=1,
            concat_axis=1,
            tiled=True,
        ),
    )
    slot_inputs = got_rows.reshape(owners, exp_dev, capacity, quarter)
    slot_grads = got_grads.reshape(owners, exp_dev, capacity, quarter)
    gate_part = jnp.einsum(
        "secd,efd->secf", slot_inputs, w_gate, preferred_element_type=jnp.float32
    )
    up_part = jnp.einsum("secd,efd->secf", slot_inputs, w_up, preferred_element_type=jnp.float32)
    grad_part = jnp.einsum("secd,efd->secf", slot_grads, w_down, preferred_element_type=jnp.float32)
    gate_share, up_share = (
        lax.psum_scatter(gate_part, "head", scatter_dimension=3, tiled=True),
        lax.psum_scatter(up_part, "head", scatter_dimension=3, tiled=True),
    )
    sigma, silu_gate, hidden_share = forward_share(gate_share, up_share)
    hidden = lax.all_gather(hidden_share, "head", axis=3, tiled=True)
    grad_share = lax.psum_scatter(grad_part, "head", scatter_dimension=3, tiled=True)
    gate_grad_share, up_grad_share = backward_share(
        grad_share, gate_share, up_share, sigma, silu_gate
    )
    gate_grad, up_grad = (
        lax.all_gather(gate_grad_share, "head", axis=3, tiled=True),
        lax.all_gather(up_grad_share, "head", axis=3, tiled=True),
    )
    expert_out = jnp.einsum(
        "secf,efd->secd", hidden, w_down, preferred_element_type=jnp.float32
    ).astype(jnp.bfloat16)
    grad_down = jnp.einsum(
        "secf,secd->efd", hidden, slot_grads, preferred_element_type=jnp.float32
    ).astype(jnp.bfloat16)
    grad_gate = jnp.einsum(
        "secf,secd->efd", gate_grad, slot_inputs, preferred_element_type=jnp.float32
    ).astype(jnp.bfloat16)
    grad_up = jnp.einsum(
        "secf,secd->efd", up_grad, slot_inputs, preferred_element_type=jnp.float32
    ).astype(jnp.bfloat16)
    returned = lax.all_to_all(
        expert_out.reshape(owners, exp_dev * capacity, quarter),
        ("ctx", "exp"),
        split_axis=0,
        concat_axis=0,
        tiled=True,
    )
    returned = returned.reshape(experts * capacity, quarter)
    picked = returned[slot_index].astype(jnp.float32) * flat_probs[:, None]
    moe_part = jnp.sum(picked.reshape(tok_rows, top_count, quarter), axis=1)
    own_state = lax.dynamic_slice_in_dim(hstate, head_index * quarter, quarter, 1)
    layer_out = (own_state + moe_part).astype(jnp.bfloat16)
    return (layer_out, grad_gate, grad_up, grad_down)


def ring_id(ctx, head, exp):
    return {"ctx": ctx, "head": head, "exp": exp}


def remote(src, dst, send_sem, recv_sem, device):
    return pltpu.make_async_remote_copy(
        src_ref=src,
        dst_ref=dst,
        send_sem=send_sem,
        recv_sem=recv_sem,
        device_id=device,
        device_id_type=MESH,
    )


def greet(devices):
    barrier = pltpu.get_barrier_semaphore()
    for device in devices:
        pl.semaphore_signal(barrier, inc=1, device_id=device, device_id_type=MESH)
    pl.semaphore_wait(barrier, len(devices))


def token_group(n_exp):
    ctx, head, exp = lax.axis_index("ctx"), lax.axis_index("head"), lax.axis_index("exp")
    others = []
    for dx in range(2):
        for dz in range(n_exp):
            if dx or dz:
                to_ctx = 1 - ctx if dx else ctx
                to_exp = lax.rem(exp + dz, n_exp)
                from_exp = lax.rem(exp + n_exp - dz, n_exp)
                others.append(
                    (dx * n_exp + dz, ring_id(to_ctx, head, to_exp), to_ctx * n_exp + to_exp,
                     to_ctx * n_exp + from_exp)
                )
    return others


class Gather:
    def __init__(self, n_exp, own, block, send_sem, recv_sem):
        self.n_exp, self.own, self.block = n_exp, own, block
        self.send_sem, self.recv_sem = send_sem, recv_sem
        self.ctx, self.head = lax.axis_index("ctx"), lax.axis_index("head")
        self.exp = lax.axis_index("exp")
        self.me = self.ctx * n_exp + self.exp
        self.across = ring_id(1 - self.ctx, self.head, self.exp)
        self.sent = []

    def start(self):
        for dz in range(1, self.n_exp):
            device = ring_id(self.ctx, self.head, lax.rem(self.exp + dz, self.n_exp))
            self.send(self.own, self.me, dz, device)
        self.send(self.own, self.me, self.n_exp, self.across)

    def send(self, source, index, sem, device):
        copy = remote(
            source, self.block(index), self.send_sem.at[sem], self.recv_sem.at[sem], device
        )
        copy.start()
        self.sent.append(copy)

    def arrived(self, index, sem):
        remote(
            self.block(index),
            self.block(index),
            self.send_sem.at[sem],
            self.recv_sem.at[sem],
            self.across,
        ).wait_recv()

    def forward(self):
        for dz in range(1, self.n_exp):
            index = self.ctx * self.n_exp + lax.rem(self.exp + self.n_exp - dz, self.n_exp)
            self.arrived(index, dz)
            self.send(self.block(index), index, self.n_exp + dz, self.across)

    def finish(self):
        other = (1 - self.ctx) * self.n_exp
        self.arrived(other + self.exp, self.n_exp)
        for dz in range(1, self.n_exp):
            self.arrived(
                other + lax.rem(self.exp + self.n_exp - dz, self.n_exp), self.n_exp + dz
            )


def layer_kernel(
    n_exp,
    capacity,
    kv_ref,
    query_ref,
    doc_ref,
    route_ref,
    prob_ref,
    cot_ref,
    weight_ref,
    resid_ref,
    gain_ref,
    gate_ref,
    up_ref,
    down_ref,
    layer_ref,
    grad_gate_ref,
    grad_up_ref,
    grad_down_ref,
    kv_all,
    cot_all,
    meta_out,
    meta_all,
    weight_all,
    attn_all,
    part_out,
    part_in,
    cols_out,
    cols_in,
    square_out,
    square_in,
    own_normed,
    normed_all,
    slot_in,
    slot_grad,
    picks,
    slot_prob,
    core_out,
    core_in,
    side_out,
    side_in,
    own_sum,
    acts,
    scaled,
    back_out,
    back_in,
    own_back,
    meta_send,
    meta_recv,
    kv_send,
    kv_recv,
    cot_send,
    cot_recv,
    weight_send,
    weight_recv,
    line_send,
    line_recv,
    part_send,
    part_recv,
    cols_send,
    cols_recv,
    square_send,
    square_recv,
    token_send,
    token_recv,
    core_send,
    core_recv,
    side_send,
    side_recv,
    act_send,
    act_recv,
    back_send,
    back_recv,
):
    ctx, head, exp = lax.axis_index("ctx"), lax.axis_index("head"), lax.axis_index("exp")
    me = ctx * n_exp + exp
    blocks, rows, quarter = normed_all.shape
    width = resid_ref.shape[1]
    experts, hidden_units = gate_ref.shape[:2]
    share = blocks * capacity // 4
    half = quarter // 2
    core_peer, side_peer = ring_id(ctx, head ^ 1, exp), ring_id(ctx, head ^ 2, exp)
    across = ring_id(1 - ctx, head, exp)
    others = token_group(n_exp)
    lane = lax.broadcasted_iota(jnp.int32, (rows, 128), 1)
    weight_of = jnp.zeros((rows, 128), F32)
    for k in range(route_ref.shape[1]):
        weight_of = weight_of + jnp.where(
            route_ref[:, k : k + 1] == lane, prob_ref[:, k : k + 1], 0.0
        )
    earlier = jnp.where(lax.broadcasted_iota(jnp.int32, (rows, 128), 0) > lane, 1.0, 0.0)
    mask = jnp.where(weight_of > 0.0, 1.0, 0.0)
    rank_of = jnp.dot(earlier.astype(BF16), mask.astype(BF16), preferred_element_type=F32)
    weight_of, rank_of = weight_of.T, rank_of.T
    doc_row = doc_ref[...].astype(F32)
    doc_column = jnp.broadcast_to(doc_row, (rows, 128)).T
    for owner in range(blocks):
        mine = slice(owner * experts, (owner + 1) * experts)
        meta_out[owner, 0:2, :] = weight_of[mine, :]
        meta_out[owner, 2:4, :] = jnp.broadcast_to(doc_row, (2, rows))
        meta_out[owner, 4:6, :] = rank_of[mine, :]
        meta_out[owner, 6:8, :] = jnp.zeros((2, rows), F32)
    greet(
        [
            ring_id(ctx, head ^ r, lax.rem(exp + dz, n_exp))
            for r in range(4)
            for dz in range(n_exp)
            if r or dz
        ]
        + [ring_id(1 - ctx, head, lax.rem(exp + dz, n_exp)) for dz in range(n_exp)]
    )
    sent = []

    def begin(copy):
        copy.start()
        sent.append(copy)

    def kv_block(index):
        return kv_all.at[:, pl.ds(pl.multiple_of(index * rows, rows), rows), :]

    kv_gather = Gather(n_exp, kv_ref, kv_block, kv_send, kv_recv)
    for sem, device, to_block, _ in others:
        begin(
            remote(
                meta_out.at[to_block], meta_all.at[me], meta_send.at[sem], meta_recv.at[sem], device
            )
        )
    kv_gather.start()
    kv_all[:, pl.ds(pl.multiple_of(me * rows, rows), rows), :] = kv_ref[...]
    meta_all[me] = meta_out[me]
    columns = pl.ds(pl.multiple_of(head * quarter, quarter), quarter)
    for sem, device, _, from_block in others:
        remote(
            meta_all.at[from_block],
            meta_all.at[from_block],
            meta_send.at[sem],
            meta_recv.at[sem],
            device,
        ).wait_recv()
    total = kv_all.shape[1]
    key_doc = jnp.concatenate([meta_all[s, 2:3, :] for s in range(total // rows)], axis=1)
    key_pos = lax.broadcasted_iota(jnp.int32, (rows, total), 1)
    query_pos = me * rows + lax.broadcasted_iota(jnp.int32, (rows, total), 0)
    visible = (key_pos <= query_pos) & (key_doc == doc_column[:, 0:1])
    kv_gather.forward()
    begin(
        remote(weight_ref, weight_all.at[ctx], weight_send.at[0], weight_recv.at[0], across)
    )
    weight_all[ctx] = weight_ref[...]
    def place(e, s):
        return pl.ds(pl.multiple_of((e * blocks + s) * capacity, 16), capacity)

    for e in range(experts):
        for s in range(blocks):
            weight, rank = meta_all[s, e : e + 1, :], meta_all[s, 4 + e : 5 + e, :]
            slot = lax.broadcasted_iota(jnp.int32, (capacity, rows), 0).astype(F32)
            pick = jnp.where((slot == rank) & (weight > 0.0), 1.0, 0.0)
            prob = jnp.sum(pick * weight, axis=1, keepdims=True)
            picks[e * blocks + s] = pick.astype(BF16)
            slot_prob[place(e, s), :] = jnp.broadcast_to(prob, (capacity, 128))

    kv_gather.finish()

    scale = HEAD_DIMENSION ** (-0.5)
    heads = query_ref.shape[1] // HEAD_DIMENSION
    chunks = 4
    chunk_lanes = query_ref.shape[1] // chunks

    def line_copy(way, c, k, receive):
        index = exp - k if way == 0 else exp + k
        view = attn_all.at[index, :, c * chunk_lanes : (c + 1) * chunk_lanes]
        first = (way * chunks + c) * n_exp
        device = ring_id(ctx, head, exp + 1 if way == 0 else exp - 1)
        if receive:
            device = across
        return remote(
            view,
            view,
            line_send.at[first + k],
            line_recv.at[first + (k if receive else k + 1)],
            device,
        )

    def holds(way, k):
        return exp >= k if way == 0 else exp <= n_exp - 1 - k

    def passes(way, k):
        return holds(way, k) & (exp < n_exp - 1 if way == 0 else exp > 0)

    def line_pass(c, k):
        for way in range(2):
            if k:

                @pl.when(holds(way, k))
                def _():
                    line_copy(way, c, k, True).wait_recv()

            if k < n_exp - 1:

                @pl.when(passes(way, k))
                def _():
                    line_copy(way, c, k, False).start()

    for c in range(chunks):
        for number in range(c * heads // chunks, (c + 1) * heads // chunks):
            lanes = slice(number * HEAD_DIMENSION, (number + 1) * HEAD_DIMENSION)
            scores = lax.dot_general(
                query_ref[:, lanes], kv_all[0], (((1,), (1,)), ((), ())), preferred_element_type=F32
            )
            scores = jnp.where(visible, scores * scale, -1e30)
            weights = jnp.exp(scores - jnp.max(scores, axis=1, keepdims=True))
            row_total = jnp.sum(weights, axis=1, keepdims=True)
            mixed = jnp.dot(weights.astype(BF16), kv_all[1], preferred_element_type=F32)
            attn_all[exp, :, lanes] = (mixed / row_total).astype(BF16)
        line_pass(c, 0)
        if c:
            line_pass(c - 1, 1)
    line_pass(chunks - 1, 1)
    for c in range(chunks):
        line_pass(c, 2)

    for c in range(chunks):
        line_pass(c, 3)
    cot_gather = Gather(
        n_exp, cot_ref.at[:, columns], lambda index: cot_all.at[index], cot_send, cot_recv
    )
    cot_gather.start()
    cot_all[me] = cot_ref[:, columns]
    weight_view = weight_all.at[1 - ctx]
    remote(
        weight_view, weight_view, weight_send.at[0], weight_recv.at[0], across
    ).wait_recv()

    def projected(index):
        block = attn_all[index]
        return jnp.concatenate(
            [jnp.dot(block, weight_all[p], preferred_element_type=F32) for p in range(2)], axis=1
        )

    part_copies = []
    for r in (2, 3, 1):
        part_out[r - 1] = projected(head ^ r).astype(BF16)
        copy = remote(
            part_out.at[r - 1],
            part_in.at[r - 1],
            part_send.at[r - 1],
            part_recv.at[r - 1],
            ring_id(ctx, head ^ r, exp),
        )
        begin(copy)
        part_copies.append(copy)
    state = projected(head)
    for copy in part_copies:
        copy.wait_recv()
    for r in range(3):
        state = state + part_in[r].astype(F32)
    side = lax.rem(exp, 2)
    for p in range(2):
        cols_out[p] = state[:, p * half : (p + 1) * half].astype(BF16)

    def cols_copy(p):
        target = 2 * p + lax.div(exp, 2)
        own = (target == head) & (head == exp)
        copy = remote(
            cols_out.at[p],
            cols_in.at[side],
            cols_send.at[p],
            cols_recv.at[side],
            ring_id(ctx, target, head),
        )
        return own, copy

    for p in range(2):
        own, copy = cols_copy(p)

        @pl.when(jnp.logical_not(own))
        def _():
            copy.start()

        @pl.when(own)
        def _():
            cols_in[side] = cols_out[p]

    for p in range(2):
        source = 2 * lax.rem(head, 2) + p
        own = (source == exp) & (head == exp)

        @pl.when(jnp.logical_not(own))
        def _():
            view = cols_in.at[p]
            remote(view, view, cols_send.at[p], cols_recv.at[p], across).wait_recv()

    state = jnp.concatenate([cols_in[0], cols_in[1]], axis=1).astype(F32)
    state = (resid_ref[:, columns].astype(F32) + state).astype(BF16)
    layer_ref[...] = state
    state = state.astype(F32)
    squares = jnp.sum(state * state, axis=1, keepdims=True)
    squares = jnp.broadcast_to(squares, (rows, 128)).T[0:8, :]
    square_out[...] = squares
    square_copies = []
    for r in (2, 3, 1):
        copy = remote(
            square_out,
            square_in.at[r - 1],
            square_send.at[r - 1],
            square_recv.at[r - 1],
            ring_id(ctx, head ^ r, exp),
        )
        begin(copy)
        square_copies.append(copy)
    cot_gather.forward()
    for copy in square_copies:
        copy.wait_recv()
    for r in range(3):
        squares = squares + square_in[r]
    inverse = lax.rsqrt(squares / width + 1e-06)
    inverse = jnp.broadcast_to(inverse[0:1, :], (rows, 128)).T[:, 0:1]
    normed = (state * inverse * gain_ref[:, columns]).astype(BF16)
    own_normed[...] = normed
    token_gather = Gather(
        n_exp, own_normed, lambda index: normed_all.at[index], token_send, token_recv
    )
    token_gather.start()
    normed_all[me] = normed

    kinds = ((slot_in, gate_ref), (slot_in, up_ref), (slot_grad, down_ref))
    def rows_of(e, index):
        return pl.ds(pl.multiple_of(e * 4 * share + index * share, 16), share)

    def own_rows(index):
        return pl.ds(pl.multiple_of(index * share, 16), share)

    def partial(kind, e, index):
        data, weight = kinds[kind]
        return lax.dot_general(
            data[rows_of(e, index), :],
            weight[e],
            (((1,), (1,)), ((), ())),
            preferred_element_type=F32,
        )

    def core_copy(kind, e):
        n = kind * experts + e
        return remote(
            core_out.at[n], core_in.at[n], core_send.at[n], core_recv.at[n], core_peer
        )

    def side_copy(kind, e):
        n = kind * experts + e
        return remote(
            side_out.at[n], side_in.at[n], side_send.at[n], side_recv.at[n], side_peer
        )

    def reduce_start(kind, e):
        n = kind * experts + e
        core_out[n, 1] = partial(kind, e, head ^ 3).astype(BF16)
        core_out[n, 0] = partial(kind, e, head ^ 1).astype(BF16)
        begin(core_copy(kind, e))
        crossing = partial(kind, e, head ^ 2)
        core_copy(kind, e).wait_recv()
        side_out[n] = (crossing + core_in[n, 1].astype(F32)).astype(BF16)
        begin(side_copy(kind, e))
        own_sum[n] = partial(kind, e, head) + core_in[n, 0].astype(F32)

    def reduced(kind, e):
        n = kind * experts + e
        side_copy(kind, e).wait_recv()
        return own_sum[n] + side_in[n].astype(F32)

    def act_copy(kind, e, index, way):
        n = kind * experts + e
        view = acts.at[n, own_rows(index), :]
        device = side_peer if way == 0 else core_peer
        return remote(view, view, act_send.at[n * 3 + way], act_recv.at[n * 3 + way], device)

    def spread(kind, e, value):
        acts[kind * experts + e, own_rows(head), :] = value
        begin(act_copy(kind, e, head, 0))
        begin(act_copy(kind, e, head, 1))

    def pass_on(kind, e):
        act_copy(kind, e, head ^ 2, 0).wait_recv()
        begin(act_copy(kind, e, head ^ 2, 2))

    def spread_done(kind, e):
        act_copy(kind, e, head ^ 1, 1).wait_recv()
        act_copy(kind, e, head ^ 3, 2).wait_recv()

    cot_gather.finish()
    for e in range(experts):
        for s in range(blocks):
            slot_grad[place(e, s), :] = (
                slot_prob[place(e, s), 0:1]
                * jnp.dot(picks[e * blocks + s], cot_all[s], preferred_element_type=F32)
            ).astype(BF16)
        reduce_start(2, e)
        if e == 0:
            token_gather.forward()
    token_gather.finish()
    for e in range(experts):
        for s in range(blocks):
            slot_in[place(e, s), :] = jnp.dot(
                picks[e * blocks + s], normed_all[s], preferred_element_type=F32
            ).astype(BF16)

        for kind in (0, 1):
            reduce_start(kind, e)
    for e in range(experts):
        gate, up = reduced(0, e), reduced(1, e)
        own_sum[e], own_sum[experts + e] = gate, up
        sigma = 1.0 / (1.0 + jnp.exp(-gate))
        spread(0, e, (gate * sigma * up).astype(BF16))

    def weight_grad(kind, e, out, data):
        n = kind * experts + e
        source = data[pl.ds(e * 4 * share, 4 * share), :]
        for first in range(0, hidden_units, 256):
            out[e, first : first + 256, :] = lax.dot_general(
                acts[n, :, first : first + 256],
                source,
                (((0,), (0,)), ((), ())),
                preferred_element_type=F32,
            ).astype(BF16)

    for e in range(experts):
        pass_on(0, e)
        grad = reduced(2, e)
        gate, up = own_sum[e], own_sum[experts + e]
        sigma = 1.0 / (1.0 + jnp.exp(-gate))
        spread(1, e, (grad * up * sigma * (1.0 + gate * (1.0 - sigma))).astype(BF16))
        spread(2, e, (grad * gate * sigma).astype(BF16))
    for e in range(experts):
        spread_done(0, e)
        for index in range(4):
            part = pl.ds(index * share, share)
            whole = pl.ds((e * 4 + index) * share, share)
            out = jnp.dot(acts[e, part, :], down_ref[e], preferred_element_type=F32)
            out = out.astype(BF16).astype(F32)
            scaled[whole, :] = (slot_prob[whole, 0:1] * out).astype(BF16)

    def combined(s):
        total = jnp.zeros((rows, quarter), F32)
        for e in range(experts):
            total = total + lax.dot_general(
                picks[e * blocks + s],
                scaled[place(e, s), :],
                (((0,), (0,)), ((), ())),
                preferred_element_type=F32,
            )
        return total.astype(BF16)

    turns = tuple(range(1, n_exp)) + (0,)
    back_copies = {}
    for dz in turns:
        to_exp = lax.rem(exp + dz, n_exp)
        back_out[dz] = combined((1 - ctx) * n_exp + to_exp)
        back_copies[dz] = remote(
            back_out.at[dz], back_in.at[dz], back_send.at[dz], back_recv.at[dz], across
        )
        begin(back_copies[dz])
    weight_grad(0, 0, grad_down_ref, slot_grad)
    total = layer_ref[...].astype(F32)
    for dz in turns:
        to_exp = lax.rem(exp + dz, n_exp)
        near = combined(ctx * n_exp + to_exp).astype(F32)
        back_copies[dz].wait_recv()
        near = near + back_in[dz].astype(F32)
        if dz == 0:
            total = total + near
            continue
        n = n_exp + dz
        back_out[n] = near.astype(BF16)
        back_copies[n] = remote(
            back_out.at[n],
            back_in.at[n],
            back_send.at[n],
            back_recv.at[n],
            ring_id(ctx, head, to_exp),
        )
        begin(back_copies[n])
    own_back[...] = total
    for e in range(1, experts):
        weight_grad(0, e, grad_down_ref, slot_grad)
    for e in range(experts):
        for kind, out in ((1, grad_gate_ref), (2, grad_up_ref)):
            pass_on(kind, e)
            spread_done(kind, e)
            weight_grad(kind, e, out, slot_in)
    total = own_back[...]
    for dz in range(1, n_exp):
        n = n_exp + dz
        back_copies[n].wait_recv()
        total = total + back_in[n].astype(F32)
    layer_ref[...] = total.astype(BF16)
    for copy in sent + kv_gather.sent + cot_gather.sent + token_gather.sent:
        copy.wait_send()
    for p in range(2):
        own, copy = cols_copy(p)

        @pl.when(jnp.logical_not(own))
        def _():
            copy.wait_send()

    for way in range(2):
        for c in range(chunks):
            for k in range(n_exp - 1):

                @pl.when(passes(way, k))
                def _():
                    line_copy(way, c, k, False).wait_send()


def per_device(
    resid,
    queries,
    rotated_key_value_pairs,
    doc_ids,
    out_weight,
    norm_gain,
    routes,
    probs,
    w_gate,
    w_up,
    w_down,
    cotangent,
):
    rows, width = resid.shape
    n_ctx, n_exp, n_head = (lax.axis_size(name) for name in ("ctx", "exp", "head"))
    experts_here, hidden_units, quarter = w_gate.shape
    owners = n_ctx * n_exp
    experts = experts_here * owners
    capacity = rows * routes.shape[1] * 5 // (4 * experts)
    if (
        n_ctx != 2
        or n_head != 4
        or n_exp != n_head
        or experts_here != 2
        or capacity % 16
        or rows != 128
        or experts > 128
        or capacity * experts_here < rows
        or rotated_key_value_pairs.shape[2] != HEAD_DIMENSION
    ):
        return per_device_slots(
            resid,
            queries,
            rotated_key_value_pairs,
            doc_ids,
            out_weight,
            norm_gain,
            routes,
            probs,
            w_gate,
            w_up,
            w_down,
            cotangent,
        )
    dma = pltpu.SemaphoreType.DMA
    vmem = pl.BlockSpec(memory_space=pltpu.VMEM)
    shape = jax.ShapeDtypeStruct

    meta_shape = (owners, 8, rows)
    total = owners * rows
    lanes = queries.shape[1]
    slots = experts_here * owners * capacity
    quarter_rows = owners * capacity // 4
    pairs = 3 * experts_here
    grad_shape = shape(w_gate.shape, BF16)
    return pl.pallas_call(
        functools.partial(layer_kernel, n_exp, capacity),
        out_shape=(shape((rows, quarter), BF16), grad_shape, grad_shape, grad_shape),
        in_specs=[vmem] * 12,
        out_specs=(vmem,) * 4,
        scratch_shapes=[
            pltpu.VMEM((2, total, HEAD_DIMENSION), BF16),
            pltpu.VMEM((owners, rows, quarter), BF16),
            pltpu.VMEM(meta_shape, F32),
            pltpu.VMEM(meta_shape, F32),
            pltpu.VMEM((2, lanes, quarter // 2), BF16),
            pltpu.VMEM((n_exp, rows, lanes), BF16),
            pltpu.VMEM((3, rows, quarter), BF16),
            pltpu.VMEM((3, rows, quarter), BF16),
            pltpu.VMEM((2, rows, quarter // 2), BF16),
            pltpu.VMEM((2, rows, quarter // 2), BF16),
            pltpu.VMEM((8, rows), F32),
            pltpu.VMEM((3, 8, rows), F32),
            pltpu.VMEM((rows, quarter), BF16),
            pltpu.VMEM((owners, rows, quarter), BF16),
            pltpu.VMEM((slots, quarter), BF16),
            pltpu.VMEM((slots, quarter), BF16),
            pltpu.VMEM((experts_here * owners, capacity, rows), BF16),
            pltpu.VMEM((slots, 128), F32),
            pltpu.VMEM((pairs, 2, quarter_rows, hidden_units), BF16),
            pltpu.VMEM((pairs, 2, quarter_rows, hidden_units), BF16),
            pltpu.VMEM((pairs, quarter_rows, hidden_units), BF16),
            pltpu.VMEM((pairs, quarter_rows, hidden_units), BF16),
            pltpu.VMEM((pairs, quarter_rows, hidden_units), F32),
            pltpu.VMEM((pairs, 4 * quarter_rows, hidden_units), BF16),
            pltpu.VMEM((slots, quarter), BF16),
            pltpu.VMEM((owners, rows, quarter), BF16),
            pltpu.VMEM((owners, rows, quarter), BF16),
            pltpu.VMEM((rows, quarter), F32),
            dma((owners,)),
            dma((owners,)),
        ]
        + [dma((2 * n_exp,))] * 4
        + [dma((1,))] * 2
        + [dma((8 * n_exp,))] * 2
        + [dma((3,))] * 2
        + [dma((2,))] * 2
        + [dma((3,))] * 2
        + [dma((2 * n_exp,))] * 2
        + [dma((pairs,))] * 4
        + [dma((3 * pairs,))] * 2
        + [dma((owners,))] * 2,
        compiler_params=pltpu.CompilerParams(
            collective_id=1, has_side_effects=True, vmem_limit_bytes=58 << 20
        ),
    )(
        rotated_key_value_pairs,
        queries,
        doc_ids,
        routes,
        probs,
        cotangent,
        out_weight,
        resid,
        norm_gain.reshape(1, width),
        w_gate,
        w_up,
        w_down,
    )


def solution(mesh):
    return jax.shard_map(
        per_device,
        mesh=mesh,
        in_specs=(
            P(("ctx", "exp"), None),
            P(("ctx", "exp"), "head"),
            P(None, ("ctx", "exp"), "head"),
            P(None, ("ctx", "exp")),
            P("head", ("ctx", "exp")),
            P(),
            P(("ctx", "exp"), None),
            P(("ctx", "exp"), None),
            P(("ctx", "exp"), None, "head"),
            P(("ctx", "exp"), None, "head"),
            P(("ctx", "exp"), None, "head"),
            P(("ctx", "exp"), None),
        ),
        out_specs=(
            P(("ctx", "exp"), "head"),
            P(("ctx", "exp"), None, "head"),
            P(("ctx", "exp"), None, "head"),
            P(("ctx", "exp"), None, "head"),
        ),
        check_vma=False,
    )
```

```python
import functools
import math

import jax
import jax.numpy as jnp
from jax import lax
from jax.experimental import pallas as pl
from jax.experimental.pallas import tpu as pltpu
from jax.sharding import PartitionSpec as P

MESH = pl.DeviceIdType.MESH
BF16 = jnp.bfloat16
F32 = jnp.float32

HEAD_DIMENSION = 128


def attend_block(
    query_block, key_rows, value_rows, query_doc, key_doc, query_pos, key_pos, score_scale
):
    scores = (
        jnp.einsum("tgrd,sgd->gtrs", query_block, key_rows, preferred_element_type=jnp.float32)
        * score_scale
    )
    visible = (key_pos[None, :] <= query_pos[:, None]) & (key_doc[None, :] == query_doc[:, None])
    visible = visible[None, :, None, :]
    scores = jnp.where(visible, scores, -1e30)
    row_max = jnp.max(scores, axis=-1, keepdims=True)
    weights = jnp.where(visible, jnp.exp(scores - row_max), 0.0)
    row_total = jnp.sum(weights, axis=-1)
    mixed = jnp.einsum(
        "gtrs,sgd->tgrd",
        weights.astype(jnp.bfloat16),
        value_rows,
        preferred_element_type=jnp.float32,
    )
    return (mixed / jnp.transpose(row_total, (1, 0, 2))[..., None]).astype(jnp.bfloat16)


def forward_share(gate_share, up_share):
    sigma = jax.nn.sigmoid(gate_share)
    silu_gate = gate_share * sigma
    return (sigma, silu_gate, (silu_gate * up_share).astype(jnp.bfloat16))


def backward_share(grad_share, gate_share, up_share, sigma, silu_gate):
    gate_grad = (grad_share * up_share * sigma * (1.0 + gate_share * (1.0 - sigma))).astype(
        jnp.bfloat16
    )
    up_grad = (grad_share * silu_gate).astype(jnp.bfloat16)
    return (gate_grad, up_grad)


def per_device_slots(
    resid,
    queries,
    rotated_key_value_pairs,
    doc_ids,
    out_weight,
    norm_gain,
    routes,
    probs,
    w_gate,
    w_up,
    w_down,
    cotangent,
):
    tok_rows, model_width = resid.shape
    top_count = routes.shape[1]
    exp_dev = w_gate.shape[0]
    n_ctx = lax.axis_size("ctx")
    n_exp = lax.axis_size("exp")
    n_head = lax.axis_size("head")
    owners = n_ctx * n_exp
    experts = exp_dev * owners
    capacity = max(2, tok_rows * top_count * 5 // (4 * experts))
    head_size = HEAD_DIMENSION
    kv_local = rotated_key_value_pairs.shape[2] // head_size
    group_width = queries.shape[1] // (head_size * kv_local)
    whole_kv, whole_doc = (
        lax.all_gather(rotated_key_value_pairs, ("ctx", "exp"), axis=1, tiled=True),
        lax.all_gather(doc_ids, ("ctx", "exp"), axis=1, tiled=True),
    )
    total_rows = whole_kv.shape[1]
    key_rows = whole_kv[0].reshape(total_rows, kv_local, head_size)
    value_rows = whole_kv[1].reshape(total_rows, kv_local, head_size)
    key_doc = whole_doc[0]
    key_pos = jnp.arange(total_rows, dtype=jnp.int32)
    query_pos = lax.axis_index(("ctx", "exp")) * tok_rows + jnp.arange(tok_rows, dtype=jnp.int32)
    query_doc = doc_ids[0]
    group_step = math.gcd(group_width, max(1, 512 // tok_rows))
    block_count = group_width // group_step
    query_blocks = jnp.moveaxis(
        queries.reshape(tok_rows, kv_local, block_count, group_step, head_size), 2, 0
    )
    score_scale = head_size ** (-0.5)

    def attend_one(query_block):
        return attend_block(
            query_block, key_rows, value_rows, query_doc, key_doc, query_pos, key_pos, score_scale
        )

    attn = lax.map(attend_one, query_blocks)
    attn = jnp.moveaxis(attn, 0, 2).reshape(tok_rows, -1)
    partial_value = jnp.dot(
        attn,
        lax.all_gather(out_weight, ("ctx", "exp"), axis=1, tiled=True),
        preferred_element_type=jnp.float32,
    )
    attn_sum = lax.psum(partial_value, "head")
    hidden_state = (resid.astype(jnp.float32) + attn_sum).astype(jnp.bfloat16)
    hstate = hidden_state.astype(jnp.float32)
    inverse = lax.rsqrt(jnp.mean(hstate * hstate, axis=-1, keepdims=True) + 1e-06)
    normed = (hstate * inverse * norm_gain).astype(jnp.bfloat16)
    flat_routes = routes.reshape(-1)
    assigned = flat_routes.shape[0]
    onehot = (flat_routes[:, None] == jnp.arange(experts, dtype=jnp.int32)[None, :]).astype(
        jnp.int32
    )
    slot_rank = jnp.sum((jnp.cumsum(onehot, axis=0) - onehot) * onehot, axis=1)
    slot_index = flat_routes * capacity + slot_rank
    slot_owner = jnp.full((experts * capacity,), assigned, jnp.int32)
    slot_owner = slot_owner.at[slot_index].set(jnp.arange(assigned, dtype=jnp.int32))
    slot_rows = slot_owner // top_count
    flat_probs = probs.reshape(-1)
    probs_pad = jnp.concatenate([flat_probs, jnp.zeros((1,), jnp.float32)])
    head_index = lax.axis_index("head")
    quarter = model_width // n_head
    source_rows = lax.dynamic_slice_in_dim(normed, head_index * quarter, quarter, 1)
    source_cot = lax.dynamic_slice_in_dim(cotangent, head_index * quarter, quarter, 1)
    rows_pad = jnp.concatenate([source_rows, jnp.zeros((1, quarter), jnp.bfloat16)], axis=0)
    cot_pad = jnp.concatenate([source_cot, jnp.zeros((1, quarter), jnp.bfloat16)], axis=0)
    send_rows = rows_pad[slot_rows].reshape(owners, exp_dev * capacity, quarter)
    send_grads = (probs_pad[slot_owner][:, None] * cot_pad[slot_rows].astype(jnp.float32)).astype(
        jnp.bfloat16
    )
    send_grads = send_grads.reshape(owners, exp_dev * capacity, quarter)
    got_rows, got_grads = (
        lax.all_to_all(
            lax.all_to_all(
                send_rows.reshape(n_ctx, n_exp, exp_dev * capacity, quarter),
                "ctx",
                split_axis=0,
                concat_axis=0,
                tiled=True,
            ),
            "exp",
            split_axis=1,
            concat_axis=1,
            tiled=True,
        ),
        lax.all_to_all(
            lax.all_to_all(
                send_grads.reshape(n_ctx, n_exp, exp_dev * capacity, quarter),
                "ctx",
                split_axis=0,
                concat_axis=0,
                tiled=True,
            ),
            "exp",
            split_axis=1,
            concat_axis=1,
            tiled=True,
        ),
    )
    slot_inputs = got_rows.reshape(owners, exp_dev, capacity, quarter)
    slot_grads = got_grads.reshape(owners, exp_dev, capacity, quarter)
    gate_part = jnp.einsum(
        "secd,efd->secf", slot_inputs, w_gate, preferred_element_type=jnp.float32
    )
    up_part = jnp.einsum("secd,efd->secf", slot_inputs, w_up, preferred_element_type=jnp.float32)
    grad_part = jnp.einsum("secd,efd->secf", slot_grads, w_down, preferred_element_type=jnp.float32)
    gate_share, up_share = (
        lax.psum_scatter(gate_part, "head", scatter_dimension=3, tiled=True),
        lax.psum_scatter(up_part, "head", scatter_dimension=3, tiled=True),
    )
    sigma, silu_gate, hidden_share = forward_share(gate_share, up_share)
    hidden = lax.all_gather(hidden_share, "head", axis=3, tiled=True)
    grad_share = lax.psum_scatter(grad_part, "head", scatter_dimension=3, tiled=True)
    gate_grad_share, up_grad_share = backward_share(
        grad_share, gate_share, up_share, sigma, silu_gate
    )
    gate_grad, up_grad = (
        lax.all_gather(gate_grad_share, "head", axis=3, tiled=True),
        lax.all_gather(up_grad_share, "head", axis=3, tiled=True),
    )
    expert_out = jnp.einsum(
        "secf,efd->secd", hidden, w_down, preferred_element_type=jnp.float32
    ).astype(jnp.bfloat16)
    grad_down = jnp.einsum(
        "secf,secd->efd", hidden, slot_grads, preferred_element_type=jnp.float32
    ).astype(jnp.bfloat16)
    grad_gate = jnp.einsum(
        "secf,secd->efd", gate_grad, slot_inputs, preferred_element_type=jnp.float32
    ).astype(jnp.bfloat16)
    grad_up = jnp.einsum(
        "secf,secd->efd", up_grad, slot_inputs, preferred_element_type=jnp.float32
    ).astype(jnp.bfloat16)
    returned = lax.all_to_all(
        expert_out.reshape(owners, exp_dev * capacity, quarter),
        ("ctx", "exp"),
        split_axis=0,
        concat_axis=0,
        tiled=True,
    )
    returned = returned.reshape(experts * capacity, quarter)
    picked = returned[slot_index].astype(jnp.float32) * flat_probs[:, None]
    moe_part = jnp.sum(picked.reshape(tok_rows, top_count, quarter), axis=1)
    own_state = lax.dynamic_slice_in_dim(hstate, head_index * quarter, quarter, 1)
    layer_out = (own_state + moe_part).astype(jnp.bfloat16)
    return (layer_out, grad_gate, grad_up, grad_down)


def ring_id(ctx, head, exp):
    return {"ctx": ctx, "head": head, "exp": exp}


def remote(src, dst, send_sem, recv_sem, device):
    return pltpu.make_async_remote_copy(
        src_ref=src,
        dst_ref=dst,
        send_sem=send_sem,
        recv_sem=recv_sem,
        device_id=device,
        device_id_type=MESH,
    )


def greet(devices):
    barrier = pltpu.get_barrier_semaphore()
    for device in devices:
        pl.semaphore_signal(barrier, inc=1, device_id=device, device_id_type=MESH)
    pl.semaphore_wait(barrier, len(devices))


def token_group(n_exp):
    ctx, head, exp = lax.axis_index("ctx"), lax.axis_index("head"), lax.axis_index("exp")
    others = []
    for dx in range(2):
        for dz in range(n_exp):
            if dx or dz:
                to_ctx = 1 - ctx if dx else ctx
                to_exp = lax.rem(exp + dz, n_exp)
                from_exp = lax.rem(exp + n_exp - dz, n_exp)
                others.append(
                    (dx * n_exp + dz, ring_id(to_ctx, head, to_exp), to_ctx * n_exp + to_exp,
                     to_ctx * n_exp + from_exp)
                )
    return others


class Gather:
    def __init__(self, n_exp, own, block, send_sem, recv_sem):
        self.n_exp, self.own, self.block = n_exp, own, block
        self.send_sem, self.recv_sem = send_sem, recv_sem
        self.ctx, self.head = lax.axis_index("ctx"), lax.axis_index("head")
        self.exp = lax.axis_index("exp")
        self.me = self.ctx * n_exp + self.exp
        self.across = ring_id(1 - self.ctx, self.head, self.exp)
        self.sent = []

    def start(self):
        for dz in range(1, self.n_exp):
            device = ring_id(self.ctx, self.head, lax.rem(self.exp + dz, self.n_exp))
            self.send(self.own, self.me, dz, device)
        self.send(self.own, self.me, self.n_exp, self.across)

    def send(self, source, index, sem, device):
        copy = remote(
            source, self.block(index), self.send_sem.at[sem], self.recv_sem.at[sem], device
        )
        copy.start()
        self.sent.append(copy)

    def arrived(self, index, sem):
        remote(
            self.block(index),
            self.block(index),
            self.send_sem.at[sem],
            self.recv_sem.at[sem],
            self.across,
        ).wait_recv()

    def forward(self):
        for dz in range(1, self.n_exp):
            index = self.ctx * self.n_exp + lax.rem(self.exp + self.n_exp - dz, self.n_exp)
            self.arrived(index, dz)
            self.send(self.block(index), index, self.n_exp + dz, self.across)

    def finish(self):
        other = (1 - self.ctx) * self.n_exp
        self.arrived(other + self.exp, self.n_exp)
        for dz in range(1, self.n_exp):
            self.arrived(
                other + lax.rem(self.exp + self.n_exp - dz, self.n_exp), self.n_exp + dz
            )


def layer_kernel(
    n_exp,
    capacity,
    kv_ref,
    query_ref,
    doc_ref,
    route_ref,
    prob_ref,
    cot_ref,
    weight_ref,
    resid_ref,
    gain_ref,
    gate_source,
    up_source,
    down_source,
    layer_ref,
    grad_gate_out,
    grad_up_out,
    grad_down_out,
    gate_ref,
    up_ref,
    down_ref,
    grad_gate_ref,
    grad_up_ref,
    grad_down_ref,
    whole,
    projections,
    kv_all,
    cot_all,
    meta_out,
    meta_all,
    weight_all,
    attn_all,
    part_out,
    part_in,
    cols_out,
    cols_in,
    square_out,
    square_in,
    own_normed,
    normed_all,
    slot_in,
    slot_grad,
    picks,
    slot_prob,
    core_out,
    core_in,
    side_out,
    side_in,
    own_sum,
    acts,
    scaled,
    back_out,
    back_in,
    own_back,
    meta_send,
    meta_recv,
    kv_send,
    kv_recv,
    cot_send,
    cot_recv,
    weight_send,
    weight_recv,
    line_send,
    line_recv,
    part_send,
    part_recv,
    cols_send,
    cols_recv,
    square_send,
    square_recv,
    token_send,
    token_recv,
    core_send,
    core_recv,
    side_send,
    side_recv,
    act_send,
    act_recv,
    back_send,
    back_recv,
    load_sem,
    store_sem,
):
    ctx, head, exp = lax.axis_index("ctx"), lax.axis_index("head"), lax.axis_index("exp")
    me = ctx * n_exp + exp
    blocks, rows, quarter = normed_all.shape
    width = resid_ref.shape[1]
    experts, hidden_units = gate_ref.shape[:2]
    share = blocks * capacity // 4
    half = quarter // 2
    core_peer, side_peer = ring_id(ctx, head ^ 1, exp), ring_id(ctx, head ^ 2, exp)
    across = ring_id(1 - ctx, head, exp)
    loads = [
        pltpu.make_async_copy(source, target, load_sem.at[n])
        for n, (source, target) in enumerate(
            ((down_source, down_ref), (gate_source, gate_ref), (up_source, up_ref))
        )
    ]
    for load in loads:
        load.start()
    others = token_group(n_exp)
    named = lax.broadcasted_iota(jnp.int32, (experts * blocks, rows), 0)
    weight_of = jnp.zeros(named.shape, F32)
    for k in range(route_ref.shape[0]):
        weight_of = weight_of + jnp.where(
            route_ref[k : k + 1, :] == named, prob_ref[k : k + 1, :], 0.0
        )
    square = (rows, rows)
    earlier = lax.broadcasted_iota(jnp.int32, square, 0) < lax.broadcasted_iota(
        jnp.int32, square, 1
    )
    mask = jnp.where(weight_of > 0.0, 1.0, 0.0)
    rank_of = jnp.dot(
        mask.astype(BF16), jnp.where(earlier, 1.0, 0.0).astype(BF16), preferred_element_type=F32
    )
    doc_row = doc_ref[...].astype(F32)
    doc_column = jnp.broadcast_to(doc_row, (rows, 128)).T
    for owner in range(blocks):
        mine = slice(owner * experts, (owner + 1) * experts)
        meta_out[owner, 0:2, :] = weight_of[mine, :]
        meta_out[owner, 2:4, :] = jnp.broadcast_to(doc_row, (2, rows))
        meta_out[owner, 4:6, :] = rank_of[mine, :]
        meta_out[owner, 6:8, :] = jnp.zeros((2, rows), F32)
    greet(
        [
            ring_id(ctx, head ^ r, lax.rem(exp + dz, n_exp))
            for r in range(4)
            for dz in range(n_exp)
            if r or dz
        ]
        + [ring_id(1 - ctx, head, lax.rem(exp + dz, n_exp)) for dz in range(n_exp)]
    )
    sent = []

    def begin(copy):
        copy.start()
        sent.append(copy)

    def kv_block(index):
        return kv_all.at[:, pl.ds(pl.multiple_of(index * rows, rows), rows), :]

    kv_gather = Gather(n_exp, kv_ref, kv_block, kv_send, kv_recv)
    for sem, device, to_block, _ in others:
        begin(
            remote(
                meta_out.at[to_block], meta_all.at[me], meta_send.at[sem], meta_recv.at[sem], device
            )
        )
    kv_gather.start()
    kv_all[:, pl.ds(pl.multiple_of(me * rows, rows), rows), :] = kv_ref[...]
    meta_all[me] = meta_out[me]
    columns = pl.ds(pl.multiple_of(head * quarter, quarter), quarter)
    for sem, device, _, from_block in others:
        remote(
            meta_all.at[from_block],
            meta_all.at[from_block],
            meta_send.at[sem],
            meta_recv.at[sem],
            device,
        ).wait_recv()
    total = kv_all.shape[1]
    key_doc = jnp.concatenate([meta_all[s, 2:3, :] for s in range(total // rows)], axis=1)
    key_pos = lax.broadcasted_iota(jnp.int32, (rows, total), 1)
    query_pos = me * rows + lax.broadcasted_iota(jnp.int32, (rows, total), 0)
    visible = (key_pos <= query_pos) & (key_doc == doc_column[:, 0:1])
    kv_gather.forward()
    begin(
        remote(weight_ref, weight_all.at[ctx], weight_send.at[0], weight_recv.at[0], across)
    )
    weight_all[ctx] = weight_ref[...]
    def place(e, s):
        return pl.ds(pl.multiple_of((e * blocks + s) * capacity, 16), capacity)

    for e in range(experts):
        for s in range(blocks):
            weight, rank = meta_all[s, e : e + 1, :], meta_all[s, 4 + e : 5 + e, :]
            slot = lax.broadcasted_iota(jnp.int32, (capacity, rows), 0).astype(F32)
            pick = jnp.where((slot == rank) & (weight > 0.0), 1.0, 0.0)
            prob = jnp.sum(pick * weight, axis=1, keepdims=True)
            picks[e * blocks + s] = pick.astype(BF16)
            slot_prob[place(e, s), :] = jnp.broadcast_to(prob, (capacity, 128))

    kv_gather.finish()

    scale = HEAD_DIMENSION ** (-0.5)
    heads = query_ref.shape[1] // HEAD_DIMENSION
    chunks = 4
    chunk_lanes = query_ref.shape[1] // chunks

    def line_copy(way, c, k, receive):
        index = exp - k if way == 0 else exp + k
        view = attn_all.at[index, :, c * chunk_lanes : (c + 1) * chunk_lanes]
        first = (way * chunks + c) * n_exp
        device = ring_id(ctx, head, exp + 1 if way == 0 else exp - 1)
        if receive:
            device = across
        return remote(
            view,
            view,
            line_send.at[first + k],
            line_recv.at[first + (k if receive else k + 1)],
            device,
        )

    def holds(way, k):
        return exp >= k if way == 0 else exp <= n_exp - 1 - k

    def passes(way, k):
        return holds(way, k) & (exp < n_exp - 1 if way == 0 else exp > 0)

    def line_pass(c, k):
        for way in range(2):
            if k:

                @pl.when(holds(way, k))
                def _():
                    line_copy(way, c, k, True).wait_recv()

            if k < n_exp - 1:

                @pl.when(passes(way, k))
                def _():
                    line_copy(way, c, k, False).start()

    for c in range(chunks):
        for number in range(c * heads // chunks, (c + 1) * heads // chunks):
            lanes = slice(number * HEAD_DIMENSION, (number + 1) * HEAD_DIMENSION)
            scores = lax.dot_general(
                query_ref[:, lanes], kv_all[0], (((1,), (1,)), ((), ())), preferred_element_type=F32
            )
            scores = jnp.where(visible, scores * scale, -1e30)
            weights = jnp.exp(scores - jnp.max(scores, axis=1, keepdims=True))
            row_total = jnp.sum(weights, axis=1, keepdims=True)
            mixed = jnp.dot(weights.astype(BF16), kv_all[1], preferred_element_type=F32)
            attn_all[exp, :, lanes] = (mixed / row_total).astype(BF16)
        line_pass(c, 0)
        if c:
            line_pass(c - 1, 1)
    line_pass(chunks - 1, 1)
    for c in range(chunks):
        line_pass(c, 2)

    for c in range(chunks):
        line_pass(c, 3)
    cot_gather = Gather(
        n_exp, cot_ref.at[:, columns], lambda index: cot_all.at[index], cot_send, cot_recv
    )
    cot_gather.start()
    cot_all[me] = cot_ref[:, columns]
    weight_view = weight_all.at[1 - ctx]
    remote(
        weight_view, weight_view, weight_send.at[0], weight_recv.at[0], across
    ).wait_recv()

    lines = attn_all[...].reshape(n_exp * rows, attn_all.shape[2])
    for p in range(2):
        projections[:, :, p * half : (p + 1) * half] = jnp.dot(
            lines, weight_all[p], preferred_element_type=F32
        ).reshape(n_exp, rows, half)

    part_copies = []
    for r in (2, 3, 1):
        part_out[r - 1] = projections[head ^ r].astype(BF16)
        copy = remote(
            part_out.at[r - 1],
            part_in.at[r - 1],
            part_send.at[r - 1],
            part_recv.at[r - 1],
            ring_id(ctx, head ^ r, exp),
        )
        begin(copy)
        part_copies.append(copy)
    state = projections[head]
    for copy in part_copies:
        copy.wait_recv()
    for r in range(3):
        state = state + part_in[r].astype(F32)
    side = lax.rem(exp, 2)
    for p in range(2):
        cols_out[p] = state[:, p * half : (p + 1) * half].astype(BF16)

    def cols_copy(p):
        target = 2 * p + lax.div(exp, 2)
        own = (target == head) & (head == exp)
        copy = remote(
            cols_out.at[p],
            cols_in.at[side],
            cols_send.at[p],
            cols_recv.at[side],
            ring_id(ctx, target, head),
        )
        return own, copy

    for p in range(2):
        own, copy = cols_copy(p)

        @pl.when(jnp.logical_not(own))
        def _():
            copy.start()

        @pl.when(own)
        def _():
            cols_in[side] = cols_out[p]

    for p in range(2):
        source = 2 * lax.rem(head, 2) + p
        own = (source == exp) & (head == exp)

        @pl.when(jnp.logical_not(own))
        def _():
            view = cols_in.at[p]
            remote(view, view, cols_send.at[p], cols_recv.at[p], across).wait_recv()

    state = jnp.concatenate([cols_in[0], cols_in[1]], axis=1).astype(F32)
    state = (resid_ref[:, columns].astype(F32) + state).astype(BF16)
    layer_ref[...] = state
    state = state.astype(F32)
    squares = jnp.sum(state * state, axis=1, keepdims=True)
    squares = jnp.broadcast_to(squares, (rows, 128)).T[0:8, :]
    square_out[...] = squares
    square_copies = []
    for r in (2, 3, 1):
        copy = remote(
            square_out,
            square_in.at[r - 1],
            square_send.at[r - 1],
            square_recv.at[r - 1],
            ring_id(ctx, head ^ r, exp),
        )
        begin(copy)
        square_copies.append(copy)
    cot_gather.forward()
    for copy in square_copies:
        copy.wait_recv()
    for r in range(3):
        squares = squares + square_in[r]
    inverse = lax.rsqrt(squares / width + 1e-06)
    inverse = jnp.broadcast_to(inverse[0:1, :], (rows, 128)).T[:, 0:1]
    normed = (state * inverse * gain_ref[:, columns]).astype(BF16)
    own_normed[...] = normed
    token_gather = Gather(
        n_exp, own_normed, lambda index: normed_all.at[index], token_send, token_recv
    )
    token_gather.start()
    normed_all[me] = normed

    kinds = ((slot_in, gate_ref), (slot_in, up_ref), (slot_grad, down_ref))
    def own_rows(index):
        return pl.ds(pl.multiple_of(index * share, 16), share)

    def partial(index):
        return whole[own_rows(index), :]

    def core_copy(kind, e):
        n = kind * experts + e
        return remote(
            core_out.at[n], core_in.at[n], core_send.at[n], core_recv.at[n], core_peer
        )

    def side_copy(kind, e):
        n = kind * experts + e
        return remote(
            side_out.at[n], side_in.at[n], side_send.at[n], side_recv.at[n], side_peer
        )

    def reduce_start(kind, e):
        n = kind * experts + e
        data, weight = kinds[kind]
        whole[...] = lax.dot_general(
            data[pl.ds(e * 4 * share, 4 * share), :],
            weight[e],
            (((1,), (1,)), ((), ())),
            preferred_element_type=F32,
        )
        core_out[n, 1] = partial(head ^ 3).astype(BF16)
        core_out[n, 0] = partial(head ^ 1).astype(BF16)
        begin(core_copy(kind, e))
        crossing = partial(head ^ 2)
        core_copy(kind, e).wait_recv()
        side_out[n] = (crossing + core_in[n, 1].astype(F32)).astype(BF16)
        begin(side_copy(kind, e))
        own_sum[n] = partial(head) + core_in[n, 0].astype(F32)

    def reduced(kind, e):
        n = kind * experts + e
        side_copy(kind, e).wait_recv()
        return own_sum[n] + side_in[n].astype(F32)

    def act_copy(kind, e, index, way):
        n = kind * experts + e
        view = acts.at[n, own_rows(index), :]
        device = side_peer if way == 0 else core_peer
        return remote(view, view, act_send.at[n * 3 + way], act_recv.at[n * 3 + way], device)

    def spread(kind, e, value):
        acts[kind * experts + e, own_rows(head), :] = value
        begin(act_copy(kind, e, head, 0))
        begin(act_copy(kind, e, head, 1))

    def pass_on(kind, e):
        act_copy(kind, e, head ^ 2, 0).wait_recv()
        begin(act_copy(kind, e, head ^ 2, 2))

    def spread_done(kind, e):
        act_copy(kind, e, head ^ 1, 1).wait_recv()
        act_copy(kind, e, head ^ 3, 2).wait_recv()

    cot_gather.finish()
    for load in loads:
        load.wait()
    for e in range(experts):
        for s in range(blocks):
            slot_grad[place(e, s), :] = (
                slot_prob[place(e, s), 0:1]
                * jnp.dot(picks[e * blocks + s], cot_all[s], preferred_element_type=F32)
            ).astype(BF16)
        reduce_start(2, e)
        if e == 0:
            token_gather.forward()
    token_gather.finish()
    for e in range(experts):
        for s in range(blocks):
            slot_in[place(e, s), :] = jnp.dot(
                picks[e * blocks + s], normed_all[s], preferred_element_type=F32
            ).astype(BF16)

        for kind in (0, 1):
            reduce_start(kind, e)
    for e in range(experts):
        gate, up = reduced(0, e), reduced(1, e)
        own_sum[e], own_sum[experts + e] = gate, up
        sigma = 1.0 / (1.0 + jnp.exp(-gate))
        spread(0, e, (gate * sigma * up).astype(BF16))

    results = ((grad_down_out, 0), (grad_gate_out, 1), (grad_up_out, 2))
    stores = []

    def weight_grad(kind, e, out, data):
        n = kind * experts + e
        source = data[pl.ds(e * 4 * share, 4 * share), :]
        for first in range(0, hidden_units, 256):
            out[e, first : first + 256, :] = lax.dot_general(
                acts[n, :, first : first + 256],
                source,
                (((0,), (0,)), ((), ())),
                preferred_element_type=F32,
            ).astype(BF16)
        target, number = results[kind]
        store = pltpu.make_async_copy(
            out.at[e], target.at[e], store_sem.at[number * experts + e]
        )
        store.start()
        stores.append(store)

    for e in range(experts):
        pass_on(0, e)
        grad = reduced(2, e)
        gate, up = own_sum[e], own_sum[experts + e]
        sigma = 1.0 / (1.0 + jnp.exp(-gate))
        spread(1, e, (grad * up * sigma * (1.0 + gate * (1.0 - sigma))).astype(BF16))
        spread(2, e, (grad * gate * sigma).astype(BF16))
    for e in range(experts):
        spread_done(0, e)
        place_all = pl.ds(e * 4 * share, 4 * share)
        out = jnp.dot(acts[e], down_ref[e], preferred_element_type=F32)
        out = out.astype(BF16).astype(F32)
        scaled[place_all, :] = (slot_prob[place_all, 0:1] * out).astype(BF16)

    def combined(s):
        total = jnp.zeros((rows, quarter), F32)
        for e in range(experts):
            total = total + lax.dot_general(
                picks[e * blocks + s],
                scaled[place(e, s), :],
                (((0,), (0,)), ((), ())),
                preferred_element_type=F32,
            )
        return total.astype(BF16)

    turns = tuple(range(1, n_exp)) + (0,)
    back_copies = {}
    for dz in turns:
        to_exp = lax.rem(exp + dz, n_exp)
        back_out[dz] = combined((1 - ctx) * n_exp + to_exp)
        back_copies[dz] = remote(
            back_out.at[dz], back_in.at[dz], back_send.at[dz], back_recv.at[dz], across
        )
        begin(back_copies[dz])
    weight_grad(0, 0, grad_down_ref, slot_grad)
    total = layer_ref[...].astype(F32)
    for dz in turns:
        to_exp = lax.rem(exp + dz, n_exp)
        near = combined(ctx * n_exp + to_exp).astype(F32)
        back_copies[dz].wait_recv()
        near = near + back_in[dz].astype(F32)
        if dz == 0:
            total = total + near
            continue
        n = n_exp + dz
        back_out[n] = near.astype(BF16)
        back_copies[n] = remote(
            back_out.at[n],
            back_in.at[n],
            back_send.at[n],
            back_recv.at[n],
            ring_id(ctx, head, to_exp),
        )
        begin(back_copies[n])
    own_back[...] = total
    for e in range(1, experts):
        weight_grad(0, e, grad_down_ref, slot_grad)
    for e in range(experts):
        for kind, out in ((1, grad_gate_ref), (2, grad_up_ref)):
            pass_on(kind, e)
            spread_done(kind, e)
            weight_grad(kind, e, out, slot_in)
    total = own_back[...]
    for dz in range(1, n_exp):
        n = n_exp + dz
        back_copies[n].wait_recv()
        total = total + back_in[n].astype(F32)
    layer_ref[...] = total.astype(BF16)
    for store in stores:
        store.wait()
    for copy in sent + kv_gather.sent + cot_gather.sent + token_gather.sent:
        copy.wait_send()
    for p in range(2):
        own, copy = cols_copy(p)

        @pl.when(jnp.logical_not(own))
        def _():
            copy.wait_send()

    for way in range(2):
        for c in range(chunks):
            for k in range(n_exp - 1):

                @pl.when(passes(way, k))
                def _():
                    line_copy(way, c, k, False).wait_send()


def per_device(
    resid,
    queries,
    rotated_key_value_pairs,
    doc_ids,
    out_weight,
    norm_gain,
    routes,
    probs,
    w_gate,
    w_up,
    w_down,
    cotangent,
):
    rows, width = resid.shape
    n_ctx, n_exp, n_head = (lax.axis_size(name) for name in ("ctx", "exp", "head"))
    experts_here, hidden_units, quarter = w_gate.shape
    owners = n_ctx * n_exp
    experts = experts_here * owners
    capacity = rows * routes.shape[1] * 5 // (4 * experts)
    if (
        n_ctx != 2
        or n_head != 4
        or n_exp != n_head
        or experts_here != 2
        or capacity % 16
        or rows != 128
        or experts > 128
        or capacity * experts_here < rows
        or rotated_key_value_pairs.shape[2] != HEAD_DIMENSION
    ):
        return per_device_slots(
            resid,
            queries,
            rotated_key_value_pairs,
            doc_ids,
            out_weight,
            norm_gain,
            routes,
            probs,
            w_gate,
            w_up,
            w_down,
            cotangent,
        )
    dma = pltpu.SemaphoreType.DMA
    vmem = pl.BlockSpec(memory_space=pltpu.VMEM)
    anywhere = pl.BlockSpec(memory_space=pl.ANY)
    shape = jax.ShapeDtypeStruct

    meta_shape = (owners, 8, rows)
    total = owners * rows
    lanes = queries.shape[1]
    slots = experts_here * owners * capacity
    quarter_rows = owners * capacity // 4
    pairs = 3 * experts_here
    grad_shape = shape(w_gate.shape, BF16)
    return pl.pallas_call(
        functools.partial(layer_kernel, n_exp, capacity),
        out_shape=(shape((rows, quarter), BF16), grad_shape, grad_shape, grad_shape),
        in_specs=[vmem] * 9 + [anywhere] * 3,
        out_specs=(vmem,) + (anywhere,) * 3,
        scratch_shapes=[pltpu.VMEM(w_gate.shape, BF16)] * 6
        + [
            pltpu.VMEM((4 * quarter_rows, hidden_units), F32),
            pltpu.VMEM((n_exp, rows, quarter), F32),
            pltpu.VMEM((2, total, HEAD_DIMENSION), BF16),
            pltpu.VMEM((owners, rows, quarter), BF16),
            pltpu.VMEM(meta_shape, F32),
            pltpu.VMEM(meta_shape, F32),
            pltpu.VMEM((2, lanes, quarter // 2), BF16),
            pltpu.VMEM((n_exp, rows, lanes), BF16),
            pltpu.VMEM((3, rows, quarter), BF16),
            pltpu.VMEM((3, rows, quarter), BF16),
            pltpu.VMEM((2, rows, quarter // 2), BF16),
            pltpu.VMEM((2, rows, quarter // 2), BF16),
            pltpu.VMEM((8, rows), F32),
            pltpu.VMEM((3, 8, rows), F32),
            pltpu.VMEM((rows, quarter), BF16),
            pltpu.VMEM((owners, rows, quarter), BF16),
            pltpu.VMEM((slots, quarter), BF16),
            pltpu.VMEM((slots, quarter), BF16),
            pltpu.VMEM((experts_here * owners, capacity, rows), BF16),
            pltpu.VMEM((slots, 128), F32),
            pltpu.VMEM((pairs, 2, quarter_rows, hidden_units), BF16),
            pltpu.VMEM((pairs, 2, quarter_rows, hidden_units), BF16),
            pltpu.VMEM((pairs, quarter_rows, hidden_units), BF16),
            pltpu.VMEM((pairs, quarter_rows, hidden_units), BF16),
            pltpu.VMEM((pairs, quarter_rows, hidden_units), F32),
            pltpu.VMEM((pairs, 4 * quarter_rows, hidden_units), BF16),
            pltpu.VMEM((slots, quarter), BF16),
            pltpu.VMEM((owners, rows, quarter), BF16),
            pltpu.VMEM((owners, rows, quarter), BF16),
            pltpu.VMEM((rows, quarter), F32),
            dma((owners,)),
            dma((owners,)),
        ]
        + [dma((2 * n_exp,))] * 4
        + [dma((1,))] * 2
        + [dma((8 * n_exp,))] * 2
        + [dma((3,))] * 2
        + [dma((2,))] * 2
        + [dma((3,))] * 2
        + [dma((2 * n_exp,))] * 2
        + [dma((pairs,))] * 4
        + [dma((3 * pairs,))] * 2
        + [dma((owners,))] * 2
        + [dma((3,)), dma((pairs,))],
        compiler_params=pltpu.CompilerParams(
            collective_id=1, has_side_effects=True, vmem_limit_bytes=58 << 20
        ),
    )(
        rotated_key_value_pairs,
        queries,
        doc_ids,
        routes.T,
        probs.T,
        cotangent,
        out_weight,
        resid,
        norm_gain.reshape(1, width),
        w_gate,
        w_up,
        w_down,
    )


def solution(mesh):
    return jax.shard_map(
        per_device,
        mesh=mesh,
        in_specs=(
            P(("ctx", "exp"), None),
            P(("ctx", "exp"), "head"),
            P(None, ("ctx", "exp"), "head"),
            P(None, ("ctx", "exp")),
            P("head", ("ctx", "exp")),
            P(),
            P(("ctx", "exp"), None),
            P(("ctx", "exp"), None),
            P(("ctx", "exp"), None, "head"),
            P(("ctx", "exp"), None, "head"),
            P(("ctx", "exp"), None, "head"),
            P(("ctx", "exp"), None),
        ),
        out_specs=(
            P(("ctx", "exp"), "head"),
            P(("ctx", "exp"), None, "head"),
            P(("ctx", "exp"), None, "head"),
            P(("ctx", "exp"), None, "head"),
        ),
        check_vma=False,
    )
```

```python
import functools
import math

import jax
import jax.numpy as jnp
from jax import lax
from jax.experimental import pallas as pl
from jax.experimental.pallas import tpu as pltpu
from jax.sharding import PartitionSpec as P

MESH = pl.DeviceIdType.MESH
BF16 = jnp.bfloat16
F32 = jnp.float32

HEAD_DIMENSION = 128


def attend_block(
    query_block, key_rows, value_rows, query_doc, key_doc, query_pos, key_pos, score_scale
):
    scores = (
        jnp.einsum("tgrd,sgd->gtrs", query_block, key_rows, preferred_element_type=jnp.float32)
        * score_scale
    )
    visible = (key_pos[None, :] <= query_pos[:, None]) & (key_doc[None, :] == query_doc[:, None])
    visible = visible[None, :, None, :]
    scores = jnp.where(visible, scores, -1e30)
    row_max = jnp.max(scores, axis=-1, keepdims=True)
    weights = jnp.where(visible, jnp.exp(scores - row_max), 0.0)
    row_total = jnp.sum(weights, axis=-1)
    mixed = jnp.einsum(
        "gtrs,sgd->tgrd",
        weights.astype(jnp.bfloat16),
        value_rows,
        preferred_element_type=jnp.float32,
    )
    return (mixed / jnp.transpose(row_total, (1, 0, 2))[..., None]).astype(jnp.bfloat16)


def forward_share(gate_share, up_share):
    sigma = jax.nn.sigmoid(gate_share)
    silu_gate = gate_share * sigma
    return (sigma, silu_gate, (silu_gate * up_share).astype(jnp.bfloat16))


def backward_share(grad_share, gate_share, up_share, sigma, silu_gate):
    gate_grad = (grad_share * up_share * sigma * (1.0 + gate_share * (1.0 - sigma))).astype(
        jnp.bfloat16
    )
    up_grad = (grad_share * silu_gate).astype(jnp.bfloat16)
    return (gate_grad, up_grad)


def per_device_slots(
    resid,
    queries,
    rotated_key_value_pairs,
    doc_ids,
    out_weight,
    norm_gain,
    routes,
    probs,
    w_gate,
    w_up,
    w_down,
    cotangent,
):
    tok_rows, model_width = resid.shape
    top_count = routes.shape[1]
    exp_dev = w_gate.shape[0]
    n_ctx = lax.axis_size("ctx")
    n_exp = lax.axis_size("exp")
    n_head = lax.axis_size("head")
    owners = n_ctx * n_exp
    experts = exp_dev * owners
    capacity = max(2, tok_rows * top_count * 5 // (4 * experts))
    head_size = HEAD_DIMENSION
    kv_local = rotated_key_value_pairs.shape[2] // head_size
    group_width = queries.shape[1] // (head_size * kv_local)
    whole_kv, whole_doc = (
        lax.all_gather(rotated_key_value_pairs, ("ctx", "exp"), axis=1, tiled=True),
        lax.all_gather(doc_ids, ("ctx", "exp"), axis=1, tiled=True),
    )
    total_rows = whole_kv.shape[1]
    key_rows = whole_kv[0].reshape(total_rows, kv_local, head_size)
    value_rows = whole_kv[1].reshape(total_rows, kv_local, head_size)
    key_doc = whole_doc[0]
    key_pos = jnp.arange(total_rows, dtype=jnp.int32)
    query_pos = lax.axis_index(("ctx", "exp")) * tok_rows + jnp.arange(tok_rows, dtype=jnp.int32)
    query_doc = doc_ids[0]
    group_step = math.gcd(group_width, max(1, 512 // tok_rows))
    block_count = group_width // group_step
    query_blocks = jnp.moveaxis(
        queries.reshape(tok_rows, kv_local, block_count, group_step, head_size), 2, 0
    )
    score_scale = head_size ** (-0.5)

    def attend_one(query_block):
        return attend_block(
            query_block, key_rows, value_rows, query_doc, key_doc, query_pos, key_pos, score_scale
        )

    attn = lax.map(attend_one, query_blocks)
    attn = jnp.moveaxis(attn, 0, 2).reshape(tok_rows, -1)
    partial_value = jnp.dot(
        attn,
        lax.all_gather(out_weight, ("ctx", "exp"), axis=1, tiled=True),
        preferred_element_type=jnp.float32,
    )
    attn_sum = lax.psum(partial_value, "head")
    hidden_state = (resid.astype(jnp.float32) + attn_sum).astype(jnp.bfloat16)
    hstate = hidden_state.astype(jnp.float32)
    inverse = lax.rsqrt(jnp.mean(hstate * hstate, axis=-1, keepdims=True) + 1e-06)
    normed = (hstate * inverse * norm_gain).astype(jnp.bfloat16)
    flat_routes = routes.reshape(-1)
    assigned = flat_routes.shape[0]
    onehot = (flat_routes[:, None] == jnp.arange(experts, dtype=jnp.int32)[None, :]).astype(
        jnp.int32
    )
    slot_rank = jnp.sum((jnp.cumsum(onehot, axis=0) - onehot) * onehot, axis=1)
    slot_index = flat_routes * capacity + slot_rank
    slot_owner = jnp.full((experts * capacity,), assigned, jnp.int32)
    slot_owner = slot_owner.at[slot_index].set(jnp.arange(assigned, dtype=jnp.int32))
    slot_rows = slot_owner // top_count
    flat_probs = probs.reshape(-1)
    probs_pad = jnp.concatenate([flat_probs, jnp.zeros((1,), jnp.float32)])
    head_index = lax.axis_index("head")
    quarter = model_width // n_head
    source_rows = lax.dynamic_slice_in_dim(normed, head_index * quarter, quarter, 1)
    source_cot = lax.dynamic_slice_in_dim(cotangent, head_index * quarter, quarter, 1)
    rows_pad = jnp.concatenate([source_rows, jnp.zeros((1, quarter), jnp.bfloat16)], axis=0)
    cot_pad = jnp.concatenate([source_cot, jnp.zeros((1, quarter), jnp.bfloat16)], axis=0)
    send_rows = rows_pad[slot_rows].reshape(owners, exp_dev * capacity, quarter)
    send_grads = (probs_pad[slot_owner][:, None] * cot_pad[slot_rows].astype(jnp.float32)).astype(
        jnp.bfloat16
    )
    send_grads = send_grads.reshape(owners, exp_dev * capacity, quarter)
    got_rows, got_grads = (
        lax.all_to_all(
            lax.all_to_all(
                send_rows.reshape(n_ctx, n_exp, exp_dev * capacity, quarter),
                "ctx",
                split_axis=0,
                concat_axis=0,
                tiled=True,
            ),
            "exp",
            split_axis=1,
            concat_axis=1,
            tiled=True,
        ),
        lax.all_to_all(
            lax.all_to_all(
                send_grads.reshape(n_ctx, n_exp, exp_dev * capacity, quarter),
                "ctx",
                split_axis=0,
                concat_axis=0,
                tiled=True,
            ),
            "exp",
            split_axis=1,
            concat_axis=1,
            tiled=True,
        ),
    )
    slot_inputs = got_rows.reshape(owners, exp_dev, capacity, quarter)
    slot_grads = got_grads.reshape(owners, exp_dev, capacity, quarter)
    gate_part = jnp.einsum(
        "secd,efd->secf", slot_inputs, w_gate, preferred_element_type=jnp.float32
    )
    up_part = jnp.einsum("secd,efd->secf", slot_inputs, w_up, preferred_element_type=jnp.float32)
    grad_part = jnp.einsum("secd,efd->secf", slot_grads, w_down, preferred_element_type=jnp.float32)
    gate_share, up_share = (
        lax.psum_scatter(gate_part, "head", scatter_dimension=3, tiled=True),
        lax.psum_scatter(up_part, "head", scatter_dimension=3, tiled=True),
    )
    sigma, silu_gate, hidden_share = forward_share(gate_share, up_share)
    hidden = lax.all_gather(hidden_share, "head", axis=3, tiled=True)
    grad_share = lax.psum_scatter(grad_part, "head", scatter_dimension=3, tiled=True)
    gate_grad_share, up_grad_share = backward_share(
        grad_share, gate_share, up_share, sigma, silu_gate
    )
    gate_grad, up_grad = (
        lax.all_gather(gate_grad_share, "head", axis=3, tiled=True),
        lax.all_gather(up_grad_share, "head", axis=3, tiled=True),
    )
    expert_out = jnp.einsum(
        "secf,efd->secd", hidden, w_down, preferred_element_type=jnp.float32
    ).astype(jnp.bfloat16)
    grad_down = jnp.einsum(
        "secf,secd->efd", hidden, slot_grads, preferred_element_type=jnp.float32
    ).astype(jnp.bfloat16)
    grad_gate = jnp.einsum(
        "secf,secd->efd", gate_grad, slot_inputs, preferred_element_type=jnp.float32
    ).astype(jnp.bfloat16)
    grad_up = jnp.einsum(
        "secf,secd->efd", up_grad, slot_inputs, preferred_element_type=jnp.float32
    ).astype(jnp.bfloat16)
    returned = lax.all_to_all(
        expert_out.reshape(owners, exp_dev * capacity, quarter),
        ("ctx", "exp"),
        split_axis=0,
        concat_axis=0,
        tiled=True,
    )
    returned = returned.reshape(experts * capacity, quarter)
    picked = returned[slot_index].astype(jnp.float32) * flat_probs[:, None]
    moe_part = jnp.sum(picked.reshape(tok_rows, top_count, quarter), axis=1)
    own_state = lax.dynamic_slice_in_dim(hstate, head_index * quarter, quarter, 1)
    layer_out = (own_state + moe_part).astype(jnp.bfloat16)
    return (layer_out, grad_gate, grad_up, grad_down)


def ring_id(ctx, head, exp):
    return {"ctx": ctx, "head": head, "exp": exp}


def remote(src, dst, send_sem, recv_sem, device):
    return pltpu.make_async_remote_copy(
        src_ref=src,
        dst_ref=dst,
        send_sem=send_sem,
        recv_sem=recv_sem,
        device_id=device,
        device_id_type=MESH,
    )


def greet(devices):
    barrier = pltpu.get_barrier_semaphore()
    for device in devices:
        pl.semaphore_signal(barrier, inc=1, device_id=device, device_id_type=MESH)
    pl.semaphore_wait(barrier, len(devices))


def token_group(n_exp):
    ctx, head, exp = lax.axis_index("ctx"), lax.axis_index("head"), lax.axis_index("exp")
    others = []
    for dx in range(2):
        for dz in range(n_exp):
            if dx or dz:
                to_ctx = 1 - ctx if dx else ctx
                to_exp = lax.rem(exp + dz, n_exp)
                from_exp = lax.rem(exp + n_exp - dz, n_exp)
                others.append(
                    (dx * n_exp + dz, ring_id(to_ctx, head, to_exp), to_ctx * n_exp + to_exp,
                     to_ctx * n_exp + from_exp)
                )
    return others


class Gather:
    def __init__(self, n_exp, own, block, send_sem, recv_sem):
        self.n_exp, self.own, self.block = n_exp, own, block
        self.send_sem, self.recv_sem = send_sem, recv_sem
        self.ctx, self.head = lax.axis_index("ctx"), lax.axis_index("head")
        self.exp = lax.axis_index("exp")
        self.me = self.ctx * n_exp + self.exp
        self.across = ring_id(1 - self.ctx, self.head, self.exp)
        self.sent = []

    def start(self):
        for dz in range(1, self.n_exp):
            device = ring_id(self.ctx, self.head, lax.rem(self.exp + dz, self.n_exp))
            self.send(self.own, self.me, dz, device)
        self.send(self.own, self.me, self.n_exp, self.across)

    def send(self, source, index, sem, device):
        copy = remote(
            source, self.block(index), self.send_sem.at[sem], self.recv_sem.at[sem], device
        )
        copy.start()
        self.sent.append(copy)

    def arrived(self, index, sem):
        remote(
            self.block(index),
            self.block(index),
            self.send_sem.at[sem],
            self.recv_sem.at[sem],
            self.across,
        ).wait_recv()

    def forward(self):
        for dz in range(1, self.n_exp):
            index = self.ctx * self.n_exp + lax.rem(self.exp + self.n_exp - dz, self.n_exp)
            self.arrived(index, dz)
            self.send(self.block(index), index, self.n_exp + dz, self.across)

    def finish(self):
        other = (1 - self.ctx) * self.n_exp
        self.arrived(other + self.exp, self.n_exp)
        for dz in range(1, self.n_exp):
            self.arrived(
                other + lax.rem(self.exp + self.n_exp - dz, self.n_exp), self.n_exp + dz
            )


def layer_kernel(
    n_exp,
    capacity,
    kv_ref,
    query_ref,
    doc_ref,
    route_ref,
    prob_ref,
    cot_ref,
    weight_ref,
    resid_ref,
    gain_ref,
    gate_source,
    up_source,
    down_source,
    layer_ref,
    grad_gate_out,
    grad_up_out,
    grad_down_out,
    gate_ref,
    up_ref,
    down_ref,
    grad_gate_ref,
    grad_up_ref,
    grad_down_ref,
    whole,
    projections,
    kv_all,
    cot_all,
    meta_out,
    meta_all,
    weight_all,
    attn_all,
    part_out,
    part_in,
    cols_out,
    cols_in,
    square_out,
    square_in,
    own_normed,
    normed_all,
    slot_in,
    slot_grad,
    picks,
    slot_prob,
    core_out,
    core_in,
    side_out,
    side_in,
    own_sum,
    acts,
    scaled,
    back_out,
    back_in,
    own_back,
    meta_send,
    meta_recv,
    kv_send,
    kv_recv,
    cot_send,
    cot_recv,
    weight_send,
    weight_recv,
    line_send,
    line_recv,
    part_send,
    part_recv,
    cols_send,
    cols_recv,
    square_send,
    square_recv,
    token_send,
    token_recv,
    core_send,
    core_recv,
    side_send,
    side_recv,
    act_send,
    act_recv,
    back_send,
    back_recv,
    load_sem,
    store_sem,
):
    ctx, head, exp = lax.axis_index("ctx"), lax.axis_index("head"), lax.axis_index("exp")
    me = ctx * n_exp + exp
    blocks, rows, quarter = normed_all.shape
    width = resid_ref.shape[1]
    experts, hidden_units = gate_ref.shape[:2]
    share = blocks * capacity // 4
    half = quarter // 2
    core_peer, side_peer = ring_id(ctx, head ^ 1, exp), ring_id(ctx, head ^ 2, exp)
    across = ring_id(1 - ctx, head, exp)
    loads = [
        pltpu.make_async_copy(source, target, load_sem.at[n])
        for n, (source, target) in enumerate(
            ((down_source, down_ref), (gate_source, gate_ref), (up_source, up_ref))
        )
    ]
    for load in loads:
        load.start()
    others = token_group(n_exp)
    named = lax.broadcasted_iota(jnp.int32, (experts * blocks, rows), 0)
    weight_of = jnp.zeros(named.shape, F32)
    for k in range(route_ref.shape[0]):
        weight_of = weight_of + jnp.where(
            route_ref[k : k + 1, :] == named, prob_ref[k : k + 1, :], 0.0
        )
    square = (rows, rows)
    earlier = lax.broadcasted_iota(jnp.int32, square, 0) < lax.broadcasted_iota(
        jnp.int32, square, 1
    )
    mask = jnp.where(weight_of > 0.0, 1.0, 0.0)
    rank_of = jnp.dot(
        mask.astype(BF16), jnp.where(earlier, 1.0, 0.0).astype(BF16), preferred_element_type=F32
    )
    doc_row = doc_ref[...].astype(F32)
    doc_column = jnp.broadcast_to(doc_row, (rows, 128)).T
    for owner in range(blocks):
        mine = slice(owner * experts, (owner + 1) * experts)
        meta_out[owner, 0:2, :] = weight_of[mine, :]
        meta_out[owner, 2:4, :] = jnp.broadcast_to(doc_row, (2, rows))
        meta_out[owner, 4:6, :] = rank_of[mine, :]
        meta_out[owner, 6:8, :] = jnp.zeros((2, rows), F32)
    greet(
        [
            ring_id(ctx, head ^ r, lax.rem(exp + dz, n_exp))
            for r in range(4)
            for dz in range(n_exp)
            if r or dz
        ]
        + [ring_id(1 - ctx, head, lax.rem(exp + dz, n_exp)) for dz in range(n_exp)]
    )
    sent = []

    def begin(copy):
        copy.start()
        sent.append(copy)

    def kv_block(index):
        return kv_all.at[:, pl.ds(pl.multiple_of(index * rows, rows), rows), :]

    kv_gather = Gather(n_exp, kv_ref, kv_block, kv_send, kv_recv)
    for sem, device, to_block, _ in others:
        begin(
            remote(
                meta_out.at[to_block], meta_all.at[me], meta_send.at[sem], meta_recv.at[sem], device
            )
        )
    kv_gather.start()
    kv_all[:, pl.ds(pl.multiple_of(me * rows, rows), rows), :] = kv_ref[...]
    meta_all[me] = meta_out[me]
    columns = pl.ds(pl.multiple_of(head * quarter, quarter), quarter)
    for sem, device, _, from_block in others:
        remote(
            meta_all.at[from_block],
            meta_all.at[from_block],
            meta_send.at[sem],
            meta_recv.at[sem],
            device,
        ).wait_recv()
    total = kv_all.shape[1]
    key_doc = jnp.concatenate([meta_all[s, 2:3, :] for s in range(total // rows)], axis=1)
    key_pos = lax.broadcasted_iota(jnp.int32, (rows, total), 1)
    query_pos = me * rows + lax.broadcasted_iota(jnp.int32, (rows, total), 0)
    visible = (key_pos <= query_pos) & (key_doc == doc_column[:, 0:1])
    kv_gather.forward()
    begin(
        remote(weight_ref, weight_all.at[ctx], weight_send.at[0], weight_recv.at[0], across)
    )
    weight_all[ctx] = weight_ref[...]
    def place(e, s):
        return pl.ds(pl.multiple_of((e * blocks + s) * capacity, 16), capacity)

    for e in range(experts):
        for s in range(blocks):
            weight, rank = meta_all[s, e : e + 1, :], meta_all[s, 4 + e : 5 + e, :]
            slot = lax.broadcasted_iota(jnp.int32, (capacity, rows), 0).astype(F32)
            pick = jnp.where((slot == rank) & (weight > 0.0), 1.0, 0.0)
            prob = jnp.sum(pick * weight, axis=1, keepdims=True)
            picks[e * blocks + s] = pick.astype(BF16)
            slot_prob[place(e, s), :] = jnp.broadcast_to(prob, (capacity, 128))

    kv_gather.finish()

    scale = HEAD_DIMENSION ** (-0.5)
    heads = query_ref.shape[1] // HEAD_DIMENSION
    chunks = 4
    chunk_lanes = query_ref.shape[1] // chunks

    def line_copy(way, c, k, receive):
        index = exp - k if way == 0 else exp + k
        view = attn_all.at[index, :, c * chunk_lanes : (c + 1) * chunk_lanes]
        first = (way * chunks + c) * n_exp
        device = ring_id(ctx, head, exp + 1 if way == 0 else exp - 1)
        if receive:
            device = across
        return remote(
            view,
            view,
            line_send.at[first + k],
            line_recv.at[first + (k if receive else k + 1)],
            device,
        )

    def holds(way, k):
        return exp >= k if way == 0 else exp <= n_exp - 1 - k

    def passes(way, k):
        return holds(way, k) & (exp < n_exp - 1 if way == 0 else exp > 0)

    def line_pass(c, k):
        for way in range(2):
            if k:

                @pl.when(holds(way, k))
                def _():
                    line_copy(way, c, k, True).wait_recv()

            if k < n_exp - 1:

                @pl.when(passes(way, k))
                def _():
                    line_copy(way, c, k, False).start()

    for c in range(chunks):
        for number in range(c * heads // chunks, (c + 1) * heads // chunks):
            lanes = slice(number * HEAD_DIMENSION, (number + 1) * HEAD_DIMENSION)
            scores = lax.dot_general(
                query_ref[:, lanes], kv_all[0], (((1,), (1,)), ((), ())), preferred_element_type=F32
            )
            scores = jnp.where(visible, scores * scale, -1e30)
            weights = jnp.exp(scores - jnp.max(scores, axis=1, keepdims=True))
            row_total = jnp.sum(weights, axis=1, keepdims=True)
            mixed = jnp.dot(weights.astype(BF16), kv_all[1], preferred_element_type=F32)
            attn_all[exp, :, lanes] = (mixed / row_total).astype(BF16)
        line_pass(c, 0)
        if c:
            line_pass(c - 1, 1)
    line_pass(chunks - 1, 1)
    for c in range(chunks):
        line_pass(c, 2)

    cot_gather = Gather(
        n_exp, cot_ref.at[:, columns], lambda index: cot_all.at[index], cot_send, cot_recv
    )
    cot_gather.start()
    cot_all[me] = cot_ref[:, columns]
    for c in range(chunks):
        line_pass(c, 3)
    weight_view = weight_all.at[1 - ctx]
    remote(
        weight_view, weight_view, weight_send.at[0], weight_recv.at[0], across
    ).wait_recv()

    lines = attn_all[...].reshape(n_exp * rows, attn_all.shape[2])
    for p in range(2):
        projections[:, :, p * half : (p + 1) * half] = jnp.dot(
            lines, weight_all[p], preferred_element_type=F32
        ).reshape(n_exp, rows, half)

    part_copies = []
    for r in (2, 3, 1):
        part_out[r - 1] = projections[head ^ r].astype(BF16)
        copy = remote(
            part_out.at[r - 1],
            part_in.at[r - 1],
            part_send.at[r - 1],
            part_recv.at[r - 1],
            ring_id(ctx, head ^ r, exp),
        )
        begin(copy)
        part_copies.append(copy)
    state = projections[head]
    for copy in part_copies:
        copy.wait_recv()
    for r in range(3):
        state = state + part_in[r].astype(F32)
    side = lax.rem(exp, 2)
    for p in range(2):
        cols_out[p] = state[:, p * half : (p + 1) * half].astype(BF16)

    def cols_copy(p):
        target = 2 * p + lax.div(exp, 2)
        own = (target == head) & (head == exp)
        copy = remote(
            cols_out.at[p],
            cols_in.at[side],
            cols_send.at[p],
            cols_recv.at[side],
            ring_id(ctx, target, head),
        )
        return own, copy

    for p in range(2):
        own, copy = cols_copy(p)

        @pl.when(jnp.logical_not(own))
        def _():
            copy.start()

        @pl.when(own)
        def _():
            cols_in[side] = cols_out[p]

    for p in range(2):
        source = 2 * lax.rem(head, 2) + p
        own = (source == exp) & (head == exp)

        @pl.when(jnp.logical_not(own))
        def _():
            view = cols_in.at[p]
            remote(view, view, cols_send.at[p], cols_recv.at[p], across).wait_recv()

    state = jnp.concatenate([cols_in[0], cols_in[1]], axis=1).astype(F32)
    state = (resid_ref[:, columns].astype(F32) + state).astype(BF16)
    layer_ref[...] = state
    state = state.astype(F32)
    squares = jnp.sum(state * state, axis=1, keepdims=True)
    squares = jnp.broadcast_to(squares, (rows, 128)).T[0:8, :]
    square_out[...] = squares
    square_copies = []
    for r in (2, 3, 1):
        copy = remote(
            square_out,
            square_in.at[r - 1],
            square_send.at[r - 1],
            square_recv.at[r - 1],
            ring_id(ctx, head ^ r, exp),
        )
        begin(copy)
        square_copies.append(copy)
    cot_gather.forward()
    for copy in square_copies:
        copy.wait_recv()
    for r in range(3):
        squares = squares + square_in[r]
    inverse = lax.rsqrt(squares / width + 1e-06)
    inverse = jnp.broadcast_to(inverse[0:1, :], (rows, 128)).T[:, 0:1]
    normed = (state * inverse * gain_ref[:, columns]).astype(BF16)
    own_normed[...] = normed
    token_gather = Gather(
        n_exp, own_normed, lambda index: normed_all.at[index], token_send, token_recv
    )
    token_gather.start()
    normed_all[me] = normed

    kinds = ((slot_in, gate_ref), (slot_in, up_ref), (slot_grad, down_ref))
    def own_rows(index):
        return pl.ds(pl.multiple_of(index * share, 16), share)

    def partial(index):
        return whole[own_rows(index), :]

    def core_copy(kind, e):
        n = kind * experts + e
        return remote(
            core_out.at[n], core_in.at[n], core_send.at[n], core_recv.at[n], core_peer
        )

    def side_copy(kind, e):
        n = kind * experts + e
        return remote(
            side_out.at[n], side_in.at[n], side_send.at[n], side_recv.at[n], side_peer
        )

    def reduce_start(kind, e):
        n = kind * experts + e
        data, weight = kinds[kind]
        whole[...] = lax.dot_general(
            data[pl.ds(e * 4 * share, 4 * share), :],
            weight[e],
            (((1,), (1,)), ((), ())),
            preferred_element_type=F32,
        )
        core_out[n, 1] = partial(head ^ 3).astype(BF16)
        core_out[n, 0] = partial(head ^ 1).astype(BF16)
        begin(core_copy(kind, e))
        crossing = partial(head ^ 2)
        core_copy(kind, e).wait_recv()
        side_out[n] = (crossing + core_in[n, 1].astype(F32)).astype(BF16)
        begin(side_copy(kind, e))
        own_sum[n] = partial(head) + core_in[n, 0].astype(F32)

    def reduced(kind, e):
        n = kind * experts + e
        side_copy(kind, e).wait_recv()
        return own_sum[n] + side_in[n].astype(F32)

    def act_copy(kind, e, index, way):
        n = kind * experts + e
        view = acts.at[n, own_rows(index), :]
        device = side_peer if way == 0 else core_peer
        return remote(view, view, act_send.at[n * 3 + way], act_recv.at[n * 3 + way], device)

    def spread(kind, e, value):
        acts[kind * experts + e, own_rows(head), :] = value
        begin(act_copy(kind, e, head, 0))
        begin(act_copy(kind, e, head, 1))

    def pass_on(kind, e):
        act_copy(kind, e, head ^ 2, 0).wait_recv()
        begin(act_copy(kind, e, head ^ 2, 2))

    def spread_done(kind, e):
        act_copy(kind, e, head ^ 1, 1).wait_recv()
        act_copy(kind, e, head ^ 3, 2).wait_recv()

    cot_gather.finish()
    for load in loads:
        load.wait()
    for e in range(experts):
        for s in range(blocks):
            slot_grad[place(e, s), :] = (
                slot_prob[place(e, s), 0:1]
                * jnp.dot(picks[e * blocks + s], cot_all[s], preferred_element_type=F32)
            ).astype(BF16)
        reduce_start(2, e)
        if e == 0:
            token_gather.forward()
    token_gather.finish()
    for e in range(experts):
        for s in range(blocks):
            slot_in[place(e, s), :] = jnp.dot(
                picks[e * blocks + s], normed_all[s], preferred_element_type=F32
            ).astype(BF16)

        for kind in (0, 1):
            reduce_start(kind, e)
    for e in range(experts):
        gate, up = reduced(0, e), reduced(1, e)
        own_sum[e], own_sum[experts + e] = gate, up
        sigma = 1.0 / (1.0 + jnp.exp(-gate))
        spread(0, e, (gate * sigma * up).astype(BF16))

    results = ((grad_down_out, 0), (grad_gate_out, 1), (grad_up_out, 2))
    stores = []

    def weight_grad(kind, e, out, data):
        n = kind * experts + e
        source = data[pl.ds(e * 4 * share, 4 * share), :]
        for first in range(0, hidden_units, 256):
            out[e, first : first + 256, :] = lax.dot_general(
                acts[n, :, first : first + 256],
                source,
                (((0,), (0,)), ((), ())),
                preferred_element_type=F32,
            ).astype(BF16)
        target, number = results[kind]
        store = pltpu.make_async_copy(
            out.at[e], target.at[e], store_sem.at[number * experts + e]
        )
        store.start()
        stores.append(store)

    for e in range(experts):
        pass_on(0, e)
        grad = reduced(2, e)
        gate, up = own_sum[e], own_sum[experts + e]
        sigma = 1.0 / (1.0 + jnp.exp(-gate))
        spread(1, e, (grad * up * sigma * (1.0 + gate * (1.0 - sigma))).astype(BF16))
        spread(2, e, (grad * gate * sigma).astype(BF16))
    for e in range(experts):
        spread_done(0, e)
        place_all = pl.ds(e * 4 * share, 4 * share)
        out = jnp.dot(acts[e], down_ref[e], preferred_element_type=F32)
        out = out.astype(BF16).astype(F32)
        scaled[place_all, :] = (slot_prob[place_all, 0:1] * out).astype(BF16)

    def combined(s):
        total = jnp.zeros((rows, quarter), F32)
        for e in range(experts):
            total = total + lax.dot_general(
                picks[e * blocks + s],
                scaled[place(e, s), :],
                (((0,), (0,)), ((), ())),
                preferred_element_type=F32,
            )
        return total.astype(BF16)

    turns = tuple(range(1, n_exp)) + (0,)
    back_copies = {}
    for dz in turns:
        to_exp = lax.rem(exp + dz, n_exp)
        back_out[dz] = combined((1 - ctx) * n_exp + to_exp)
        back_copies[dz] = remote(
            back_out.at[dz], back_in.at[dz], back_send.at[dz], back_recv.at[dz], across
        )
        begin(back_copies[dz])
    weight_grad(0, 0, grad_down_ref, slot_grad)
    total = layer_ref[...].astype(F32)
    for dz in turns:
        to_exp = lax.rem(exp + dz, n_exp)
        near = combined(ctx * n_exp + to_exp).astype(F32)
        back_copies[dz].wait_recv()
        near = near + back_in[dz].astype(F32)
        if dz == 0:
            total = total + near
            continue
        n = n_exp + dz
        back_out[n] = near.astype(BF16)
        back_copies[n] = remote(
            back_out.at[n],
            back_in.at[n],
            back_send.at[n],
            back_recv.at[n],
            ring_id(ctx, head, to_exp),
        )
        begin(back_copies[n])
    own_back[...] = total
    for e in range(1, experts):
        weight_grad(0, e, grad_down_ref, slot_grad)
    for e in range(experts):
        for kind, out in ((1, grad_gate_ref), (2, grad_up_ref)):
            pass_on(kind, e)
            spread_done(kind, e)
            weight_grad(kind, e, out, slot_in)
    total = own_back[...]
    for dz in range(1, n_exp):
        n = n_exp + dz
        back_copies[n].wait_recv()
        total = total + back_in[n].astype(F32)
    layer_ref[...] = total.astype(BF16)
    for store in stores:
        store.wait()
    for copy in sent + kv_gather.sent + cot_gather.sent + token_gather.sent:
        copy.wait_send()
    for p in range(2):
        own, copy = cols_copy(p)

        @pl.when(jnp.logical_not(own))
        def _():
            copy.wait_send()

    for way in range(2):
        for c in range(chunks):
            for k in range(n_exp - 1):

                @pl.when(passes(way, k))
                def _():
                    line_copy(way, c, k, False).wait_send()


def per_device(
    resid,
    queries,
    rotated_key_value_pairs,
    doc_ids,
    out_weight,
    norm_gain,
    routes,
    probs,
    w_gate,
    w_up,
    w_down,
    cotangent,
):
    rows, width = resid.shape
    n_ctx, n_exp, n_head = (lax.axis_size(name) for name in ("ctx", "exp", "head"))
    experts_here, hidden_units, quarter = w_gate.shape
    owners = n_ctx * n_exp
    experts = experts_here * owners
    capacity = rows * routes.shape[1] * 5 // (4 * experts)
    if (
        n_ctx != 2
        or n_head != 4
        or n_exp != n_head
        or experts_here != 2
        or capacity % 16
        or rows != 128
        or experts > 128
        or capacity * experts_here < rows
        or rotated_key_value_pairs.shape[2] != HEAD_DIMENSION
    ):
        return per_device_slots(
            resid,
            queries,
            rotated_key_value_pairs,
            doc_ids,
            out_weight,
            norm_gain,
            routes,
            probs,
            w_gate,
            w_up,
            w_down,
            cotangent,
        )
    dma = pltpu.SemaphoreType.DMA
    vmem = pl.BlockSpec(memory_space=pltpu.VMEM)
    anywhere = pl.BlockSpec(memory_space=pl.ANY)
    shape = jax.ShapeDtypeStruct

    meta_shape = (owners, 8, rows)
    total = owners * rows
    lanes = queries.shape[1]
    slots = experts_here * owners * capacity
    quarter_rows = owners * capacity // 4
    pairs = 3 * experts_here
    grad_shape = shape(w_gate.shape, BF16)
    return pl.pallas_call(
        functools.partial(layer_kernel, n_exp, capacity),
        out_shape=(shape((rows, quarter), BF16), grad_shape, grad_shape, grad_shape),
        in_specs=[vmem] * 9 + [anywhere] * 3,
        out_specs=(vmem,) + (anywhere,) * 3,
        scratch_shapes=[pltpu.VMEM(w_gate.shape, BF16)] * 6
        + [
            pltpu.VMEM((4 * quarter_rows, hidden_units), F32),
            pltpu.VMEM((n_exp, rows, quarter), F32),
            pltpu.VMEM((2, total, HEAD_DIMENSION), BF16),
            pltpu.VMEM((owners, rows, quarter), BF16),
            pltpu.VMEM(meta_shape, F32),
            pltpu.VMEM(meta_shape, F32),
            pltpu.VMEM((2, lanes, quarter // 2), BF16),
            pltpu.VMEM((n_exp, rows, lanes), BF16),
            pltpu.VMEM((3, rows, quarter), BF16),
            pltpu.VMEM((3, rows, quarter), BF16),
            pltpu.VMEM((2, rows, quarter // 2), BF16),
            pltpu.VMEM((2, rows, quarter // 2), BF16),
            pltpu.VMEM((8, rows), F32),
            pltpu.VMEM((3, 8, rows), F32),
            pltpu.VMEM((rows, quarter), BF16),
            pltpu.VMEM((owners, rows, quarter), BF16),
            pltpu.VMEM((slots, quarter), BF16),
            pltpu.VMEM((slots, quarter), BF16),
            pltpu.VMEM((experts_here * owners, capacity, rows), BF16),
            pltpu.VMEM((slots, 128), F32),
            pltpu.VMEM((pairs, 2, quarter_rows, hidden_units), BF16),
            pltpu.VMEM((pairs, 2, quarter_rows, hidden_units), BF16),
            pltpu.VMEM((pairs, quarter_rows, hidden_units), BF16),
            pltpu.VMEM((pairs, quarter_rows, hidden_units), BF16),
            pltpu.VMEM((pairs, quarter_rows, hidden_units), F32),
            pltpu.VMEM((pairs, 4 * quarter_rows, hidden_units), BF16),
            pltpu.VMEM((slots, quarter), BF16),
            pltpu.VMEM((owners, rows, quarter), BF16),
            pltpu.VMEM((owners, rows, quarter), BF16),
            pltpu.VMEM((rows, quarter), F32),
            dma((owners,)),
            dma((owners,)),
        ]
        + [dma((2 * n_exp,))] * 4
        + [dma((1,))] * 2
        + [dma((8 * n_exp,))] * 2
        + [dma((3,))] * 2
        + [dma((2,))] * 2
        + [dma((3,))] * 2
        + [dma((2 * n_exp,))] * 2
        + [dma((pairs,))] * 4
        + [dma((3 * pairs,))] * 2
        + [dma((owners,))] * 2
        + [dma((3,)), dma((pairs,))],
        compiler_params=pltpu.CompilerParams(
            collective_id=1, has_side_effects=True, vmem_limit_bytes=58 << 20
        ),
    )(
        rotated_key_value_pairs,
        queries,
        doc_ids,
        routes.T,
        probs.T,
        cotangent,
        out_weight,
        resid,
        norm_gain.reshape(1, width),
        w_gate,
        w_up,
        w_down,
    )


def solution(mesh):
    return jax.shard_map(
        per_device,
        mesh=mesh,
        in_specs=(
            P(("ctx", "exp"), None),
            P(("ctx", "exp"), "head"),
            P(None, ("ctx", "exp"), "head"),
            P(None, ("ctx", "exp")),
            P("head", ("ctx", "exp")),
            P(),
            P(("ctx", "exp"), None),
            P(("ctx", "exp"), None),
            P(("ctx", "exp"), None, "head"),
            P(("ctx", "exp"), None, "head"),
            P(("ctx", "exp"), None, "head"),
            P(("ctx", "exp"), None),
        ),
        out_specs=(
            P(("ctx", "exp"), "head"),
            P(("ctx", "exp"), None, "head"),
            P(("ctx", "exp"), None, "head"),
            P(("ctx", "exp"), None, "head"),
        ),
        check_vma=False,
    )
```
